256 devices in a mesh: exp: 2 (over z_lo), tile: 8 (over x, core), depth: 16 (over y, z_hi).
Axes of the slice: x: 4, y: 4, z: 8 (z_hi: 4, z_lo: 2; z = z_hi * 2 + z_lo), core: 2. Of those that a mesh axis runs over, the one named last changes fastest.
Arguments:
- images: float32 [2, 4, 1024, 512], P('exp', None, 'tile'), may hold values from 0.25 to 4
- offsets: int32 [4, 64], P(None, 'depth'), may hold values from -6 to 6
- fractions: float32 [4, 64], P(None, 'depth'), may hold values from 0 to 1
- shifts: int32 [128, 3], P(('tile', 'depth')), may hold values from -8 to 7
Outputs:
- correlation: float32 [128, 64, 4096], P(('tile', 'depth'), 'exp')
The draws below stay inside these ranges and needn't reach their ends.
All inputs are finite; a program needn't handle non-finite values.
Results may differ from the reference program's by a relative error of at most 0.0003.
Values sent between devices are 32-bit elements; how exact they have to be, the bound alone decides.
A program may use at most 64 MiB of HBM per device.

```python
import math
import jax
import jax.numpy as jnp
from jax import lax

CAMS = 4
BRICK = 64
ITERS = 2
NX = 1024
NY = 512
NZ = 64
NBR = 128


def draw_offsets(key, part):
    slope_key = jax.random.fold_in(key, 11)
    jitter_key = jax.random.fold_in(key, 23)
    slopes = jax.random.permutation(slope_key, jnp.array([-2, -1, 1, 2], jnp.int32))
    depth_pos = jnp.arange(NZ).astype(jnp.int32)
    base = slopes[:, None] * 3 * (2 * depth_pos[None, :] - NZ + 1) // (NZ - 1)
    jitter = jax.random.randint(jitter_key, (CAMS, NZ), -1, 2).astype(jnp.int32)
    interior = ((depth_pos > 0) & (depth_pos < NZ - 1)).astype(jnp.int32)
    return jnp.clip(base + jitter * interior[None, :], -6, 6).astype(jnp.int32)


def touch_ends(drawn, own_key, smallest, largest):
    shape = drawn.shape
    spot = [jax.random.randint(jax.random.fold_in(own_key, axis), (), 0, shape[axis]) for axis in range(len(shape))]
    drawn = drawn.at[tuple(spot)].set(smallest)
    longest = shape.index(max(shape))
    spot[longest] = (spot[longest] + 1) % shape[longest]
    return drawn.at[tuple(spot)].set(largest)


def steps_of(rng, extent, cuts, low, largest):
    def one(dim, blocks):
        draws = jax.random.uniform(jax.random.fold_in(jax.random.fold_in(rng, 6), dim), (blocks,), jnp.float32, low / len(cuts), largest / len(cuts))
        return jnp.repeat(jnp.exp(draws), extent[dim] // blocks).reshape((-1,) + (1,) * (len(extent) - dim - 1))

    loudness = one(*cuts[0])
    for cut in cuts[1:]:
        loudness = loudness * one(*cut)
    return loudness


def setup_inputs(seed: int = 0) -> dict:
    streams_of = jax.random.split(jax.random.key(seed), 5)
    images = jnp.clip(jnp.exp(math.log(4.0) - 2.7725887 * jax.random.uniform(streams_of[0], (2, CAMS, NX, NY), jnp.float32) ** steps_of(streams_of[0], (2, CAMS, NX, NY), ((0, 2), (2, 8)), -0.2, 0.2)), 0.25, 4.0)
    offsets = draw_offsets(jax.random.fold_in(streams_of[4], 71), 0)
    fractions = jnp.clip(1.0 * jax.random.uniform(streams_of[2], (CAMS, NZ), jnp.float32) ** steps_of(streams_of[2], (CAMS, NZ), ((1, 16),), -0.2, 0.2), 0.0, 1.0)
    shifts = touch_ends(jax.random.randint(streams_of[3], (NBR, 3), -8, 8), jax.random.fold_in(streams_of[3], 1), -8, 7).astype(jnp.int32)
    return dict(images=images, offsets=offsets, fractions=fractions, shifts=shifts)


def tent_weights(fractions):
    tap_list = jnp.arange(-2, 4).astype(jnp.float32)
    weights = jnp.maximum(0.0, 1.0 - jnp.abs(tap_list - fractions[..., None]) / 1.5)
    return weights / jnp.sum(weights, axis=-1, keepdims=True)


def project(volume, offsets, tent):
    tap_int = jnp.arange(-2, 4).astype(jnp.int32)
    columns = jnp.arange(NX).astype(jnp.int32)

    def z_step(total, depth_index):
        index_map = jnp.mod(columns[None, None, :] - offsets[:, depth_index][:, None, None] - tap_int[None, :, None], NX)
        gathered = jnp.take(volume[depth_index], index_map, axis=0)
        total = total + jnp.sum(tent[:, depth_index, :, None, None] * gathered, axis=1)
        return total, None

    start = jnp.zeros((CAMS, NX, NY), jnp.float32)
    total, _ = lax.scan(z_step, start, jnp.arange(NZ).astype(jnp.int32))
    return total / NZ


def backproject(ratio, offsets, tent):
    tap_int = jnp.arange(-2, 4).astype(jnp.int32)
    columns = jnp.arange(NX).astype(jnp.int32)
    cameras = jnp.arange(CAMS).astype(jnp.int32)

    def per_slab(depth_index):
        index_map = jnp.mod(columns[None, None, :] + offsets[:, depth_index][:, None, None] + tap_int[None, :, None], NX)
        gathered = ratio[cameras[:, None, None], index_map]
        return jnp.sum(tent[:, depth_index, :, None, None] * gathered, axis=(0, 1)) / CAMS

    return lax.map(per_slab, jnp.arange(NZ).astype(jnp.int32))


def reconstruct(image_set, offsets, tent):
    log_images = jnp.log(image_set)
    log_volume = jnp.zeros((NZ, NX, NY), jnp.float32)
    for iteration in range(ITERS):
        volume = jnp.exp(log_volume)
        ratio = log_images - jnp.log(project(volume, offsets, tent))
        log_volume = log_volume + backproject(ratio, offsets, tent)
    return jnp.exp(log_volume)


def to_bricks(volume):
    shaped = volume.reshape(NZ, NX // BRICK, BRICK, NY // BRICK, BRICK)
    return shaped.transpose(1, 3, 0, 2, 4).reshape(-1, BRICK, BRICK, BRICK)


def reference(images, offsets, fractions, shifts):
    tent = tent_weights(fractions)
    first = to_bricks(reconstruct(images[0], offsets, tent))
    second = to_bricks(reconstruct(images[1], offsets, tent))
    wave = jnp.arange(BRICK).astype(jnp.int32)

    def per_brick(inputs):
        brick_one, brick_two, shift_row = inputs
        spec_one = jnp.fft.fftn(brick_one, norm="ortho")
        spec_two = jnp.fft.fftn(brick_two, norm="ortho")
        turns = (wave[:, None, None] * shift_row[0] + wave[None, :, None] * shift_row[1] + wave[None, None, :] * shift_row[2]) % BRICK
        angle = turns.astype(jnp.float32) * (2.0 * math.pi / BRICK)
        scale = jnp.maximum(jnp.abs(spec_one) * jnp.abs(spec_two), 0.01)
        cross = jnp.conj(spec_one) * spec_two * (jnp.cos(angle) + 1j * jnp.sin(angle)) / scale
        anchor = (wave[:, None, None] == 0) & (wave[None, :, None] == 0) & (wave[None, None, :] == 0)
        cross = jnp.where(anchor, jnp.zeros_like(cross), cross)
        result = jnp.real(jnp.fft.ifftn(cross, norm="ortho"))
        return result.reshape(BRICK, BRICK * BRICK).astype(jnp.float32)

    return lax.map(per_brick, (first, second, shifts))
```

```python
import functools
import math

import jax
import jax.numpy as jnp
import ml_dtypes
import numpy as np
from jax import lax
from jax.experimental import pallas as pl
from jax.experimental.pallas import tpu as pltpu
from jax.sharding import PartitionSpec as P

MESH = pl.DeviceIdType.MESH
BRICK = 64
LANES = 128
EDGE = 24
COLS_R = BRICK + 2 * EDGE
COLS_V = BRICK + 32
COLS_U = BRICK + 16
MAIN = BRICK + EDGE
PEERS = 16
FLOOR = 0.01
F32 = jnp.float32
BF16 = jnp.bfloat16


def exchange_kernel(off_ref, frac_ref, img_ref, raw_ref, par_ref, tile_ref, par_send, par_recv, send, recv, local):
    e = lax.axis_index("exp")
    t = lax.axis_index("tile")
    d = lax.axis_index("depth")
    tiles = lax.axis_size("tile")
    other = 1 - e
    half = d // 8
    d_far = (d // 4) * 4 + lax.rem(lax.rem(d, 4) + 3 - 2 * e, 4)
    t_to = lax.rem(t + 1 - 2 * half + tiles, tiles)
    t_from = lax.rem(t - 1 + 2 * half + tiles, tiles)

    def lanes_of(depth):
        return pl.ds(pl.multiple_of(lax.rem(depth, 8) // 2 * LANES, LANES), LANES)

    barrier = pltpu.get_barrier_semaphore()
    partners = [(e, t, lax.rem(d + k, PEERS)) for k in range(1, PEERS)]
    partners += [(other, t, d), (other, t, d_far)]
    partners += [(e, t_to, d), (other, t_to, d), (e, t_from, d), (other, t_from, d)]
    for partner in partners:
        pl.semaphore_signal(barrier, inc=1, device_id=partner, device_id_type=MESH)

    main_src = pl.ds(pl.multiple_of((BRICK - EDGE) * half, 8), MAIN)
    main_dst = pl.ds(pl.multiple_of(EDGE * (1 - half), 8), MAIN)
    strip_src = pl.ds(pl.multiple_of((2 * BRICK - EDGE) * (1 - half), 8), EDGE)
    strip_dst = pl.ds(pl.multiple_of(MAIN * half, 8), EDGE)

    own = pltpu.make_async_copy(
        img_ref.at[0, :, main_src, lanes_of(d)], raw_ref.at[e, :, main_dst, :], local.at[0]
    )
    own.start()

    row = lax.broadcasted_iota(jnp.int32, (8, LANES), 0)
    cam = lax.broadcasted_iota(jnp.int32, (8, LANES), 1) % 4
    tile = jnp.zeros((8, LANES), F32)
    for c in range(4):
        for z in range(4):
            tile = jnp.where((row == z) & (cam == c), off_ref[c, z].astype(F32), tile)
            tile = jnp.where((row == z + 4) & (cam == c), frac_ref[c, z], tile)
    tile_ref[...] = tile

    own_par = pltpu.make_async_copy(tile_ref, par_ref.at[d], local.at[1])
    own_par.start()

    pl.semaphore_wait(barrier, len(partners))

    copies = []
    for index, (target_e, target_d) in enumerate([(e, d), (other, d)]):
        copies.append(
            pltpu.make_async_remote_copy(
                src_ref=img_ref.at[0, :, strip_src, lanes_of(target_d)],
                dst_ref=raw_ref.at[e, :, strip_dst, :],
                send_sem=send.at[2 + index],
                recv_sem=recv.at[2 + index],
                device_id=(target_e, t_to, target_d),
                device_id_type=MESH,
            )
        )
    for index, target_d in enumerate([d, d_far]):
        cams = pl.ds(2 * index, 2)
        copies.append(
            pltpu.make_async_remote_copy(
                src_ref=img_ref.at[0, cams, main_src, lanes_of(target_d)],
                dst_ref=raw_ref.at[e, cams, main_dst, :],
                send_sem=send.at[index],
                recv_sem=recv.at[index],
                device_id=(other, t, target_d),
                device_id_type=MESH,
            )
        )
    for k in range(1, PEERS):
        copies.append(
            pltpu.make_async_remote_copy(
                src_ref=tile_ref,
                dst_ref=par_ref.at[d],
                send_sem=par_send.at[k],
                recv_sem=par_recv.at[k],
                device_id=(e, t, lax.rem(d + k, PEERS)),
                device_id_type=MESH,
            )
        )
    for copy in copies:
        copy.start()
    own.wait()
    own_par.wait()
    for copy in copies:
        copy.wait()


def exchange(images, offsets, fractions):
    smem = pl.BlockSpec(memory_space=pltpu.SMEM)
    anywhere = pl.BlockSpec(memory_space=pl.ANY)
    return pl.pallas_call(
        exchange_kernel,
        out_shape=[
            jax.ShapeDtypeStruct((2, 4, COLS_R, LANES), F32),
            jax.ShapeDtypeStruct((PEERS, 8, LANES), F32),
        ],
        in_specs=[smem, smem, anywhere],
        out_specs=[anywhere, anywhere],
        scratch_shapes=[
            pltpu.VMEM((8, LANES), F32),
            pltpu.SemaphoreType.DMA((PEERS,)),
            pltpu.SemaphoreType.DMA((PEERS,)),
            pltpu.SemaphoreType.DMA((4,)),
            pltpu.SemaphoreType.DMA((4,)),
            pltpu.SemaphoreType.DMA((2,)),
        ],
        compiler_params=pltpu.CompilerParams(collective_id=0, has_side_effects=True),
    )(offsets, fractions, images)


def split(value):
    high = value.astype(BF16)
    low = (value - high.astype(F32)).astype(BF16)
    return high, low


def stack_rows(value):
    high, low = split(value)
    return jnp.concatenate([high, low, high], axis=0)


def stack_lanes(value):
    high, low = split(value)
    return jnp.concatenate([high, low, high], axis=1)


def twice(value):
    high, low = split(value)
    return jnp.concatenate([high, low[:, :BRICK]], axis=1)


def dot(left, right):
    return jnp.dot(left, right, preferred_element_type=F32)


def turn_cos(turns):
    return jnp.cos((turns & (BRICK - 1)).astype(F32) * (2.0 * math.pi / BRICK)) * 0.125


def iota(shape, axis):
    return lax.broadcasted_iota(jnp.int32, shape, axis)


def compute_kernel(
    shift_ref, raw_ref, par_ref, fz_ref, ty_ref, cs_ref, out_ref, r8, rh, rl, g, a8, uh, ul, zs, qs
):
    e = lax.axis_index("exp")
    odd = lax.rem(lax.axis_index("depth"), 2)
    sz, sx, sy = shift_ref[0, 0], shift_ref[0, 1], shift_ref[0, 2]

    r = iota((2 * BRICK, LANES), 0)
    c = iota((2 * BRICK, LANES), 1)
    inv_y = turn_cos((r % BRICK) * (c % BRICK + sy) + 16 * (r // BRICK - c // BRICK))
    y_high, y_low = split(inv_y)
    tiy = jnp.concatenate([y_high, y_high, y_low], axis=0)
    x_of = 2 * (r % (BRICK // 2)) + (r % BRICK) // (BRICK // 2)
    tix = twice(turn_cos((c % BRICK) * (x_of + sx) - 16 * (r // BRICK)))
    r = iota((BRICK // 2, LANES), 0)
    c = iota((BRICK // 2, LANES), 1) % BRICK
    kz = jnp.where(c > 32, c - 32, c)
    weight = jnp.where((kz == 0) | (kz == 32), 1.0, 2.0)
    tiz = twice(weight * turn_cos(kz * (r + 32 * e + sz) + jnp.where(c > 32, 16, 0)))

    sub = iota((8, LANES), 0)
    offs, fracs = [], []
    for i in range(PEERS // 2):
        a, b = par_ref[2 * i], par_ref[2 * i + 1]
        offs.append(jnp.where(sub < 4, a, pltpu.roll(b, 4, 0)))
        fracs.append(jnp.where(sub < 4, pltpu.roll(a, 4, 0), b))
    off = jnp.concatenate(offs, axis=0)
    frac = jnp.concatenate(fracs, axis=0)
    s_of = iota((BRICK, LANES), 1) % BRICK // 4 - 7

    def tent(distance):
        return jnp.maximum(0.0, 1.0 - jnp.abs(distance - frac) / 1.5)

    total = tent(-2.0)
    for tap in range(-1, 4):
        total = total + tent(float(tap))
    weights = tent(s_of.astype(F32) - off) / total * 0.25
    back = twice(weights)
    turned = jnp.concatenate([weights, weights], axis=0).T[:BRICK] * 0.0625
    forward = twice(turned)
    ones = jnp.sum(turned[:, :BRICK], axis=1, keepdims=True)
    first = ones[0:8]
    for i in range(1, 8):
        first = first + ones[8 * i : 8 * i + 8]
    first = first + pltpu.roll(jnp.broadcast_to(first, (8, LANES)), 4, 0)
    log_first = jnp.log(first)

    low_lane = iota((COLS_R, LANES), 1) < BRICK
    pick = low_lane != (odd == 1)
    is_odd = odd == 1
    for cam in range(4):
        one, two = raw_ref[0, cam], raw_ref[1, cam]
        kept = jnp.where(is_odd, two, one)
        moved = jnp.where(is_odd, one, two)
        both = jnp.where(pick, kept, pltpu.roll(moved, BRICK, 1))
        ratio = jnp.log(both) - log_first[cam : cam + 1, :]
        r8[cam * COLS_R : (cam + 1) * COLS_R, :] = ratio
        r8[(cam + 4) * COLS_R : (cam + 5) * COLS_R, :] = pltpu.roll(ratio, COLS_R - 1, 0)

    for x in range(COLS_R - 2):
        col = jnp.concatenate(
            [r8[pl.ds(x, 8, stride=COLS_R), :], r8[pl.ds(x + 2, 8, stride=COLS_R), :]], axis=0
        )
        high, low = split(col)
        rh[:, x * LANES : (x + 1) * LANES] = high
        rl[:, x * LANES : (x + 1) * LANES] = low

    def windows(high_ref, low_ref, x):
        def of(ref):
            return [ref[:, pl.ds(pl.multiple_of((x + 1 + 4 * q) * LANES, LANES), 2 * LANES)] for q in range(4)]

        high = of(high_ref)
        return jnp.concatenate(high + of(low_ref) + high, axis=0)

    def second(i, carry):
        x = 2 * i
        volume = jnp.exp(dot(back, windows(rh, rl, x)))
        g[:, pl.ds(pl.multiple_of(x * LANES, LANES), 2 * LANES)] = dot(forward, stack_rows(volume))
        return carry

    lax.fori_loop(0, COLS_V // 2, second, 0)

    chunk = 8
    for u in range(0, COLS_U, chunk):
        n = (chunk + 1) * LANES

        def group(row, shift):
            total = None
            for q in range(4):
                start = (u + shift + 12 - 4 * q) * LANES
                part = g[16 * q + row : 16 * q + row + 8, start : start + n]
                total = part if total is None else total + part
            return total

        pairs = group(0, 2) + group(8, 0)
        proj = pairs[:, LANES:] + pltpu.roll(pairs[:, : chunk * LANES], 4, 0)
        log_proj = jnp.log(proj)
        for i in range(chunk):
            ratio = r8[pl.ds(u + i + 16, 8, stride=COLS_R), :]
            a8[:, (u + i) * LANES : (u + i + 1) * LANES] = (
                2.0 * ratio + log_first - log_proj[:, i * LANES : (i + 1) * LANES]
            )

    def column(u):
        return a8[:, u * LANES : (u + 1) * LANES]

    def pair(u):
        return jnp.where(sub < 4, column(u), pltpu.roll(column(u + 1), 4, 0))

    for u in range(COLS_U - 3):
        high, low = split(jnp.concatenate([pair(u), pair(u + 2)], axis=0))
        uh[:, u * LANES : (u + 1) * LANES] = high
        ul[:, u * LANES : (u + 1) * LANES] = low

    fz = fz_ref[...]

    def third(i, carry):
        x = 2 * i
        volume = jnp.exp(dot(back, windows(uh, ul, x)))
        spec = dot(fz, stack_rows(volume))
        start = pl.multiple_of(x * BRICK, BRICK)
        zs[pl.ds(start, BRICK), :] = spec[:, :LANES]
        zs[pl.ds(start + BRICK, BRICK), :] = spec[:, LANES:]
        return carry

    lax.fori_loop(0, BRICK // 2, third, 0)

    ty = ty_ref[...]
    cs = cs_ref[...]
    low_half = iota((BRICK, LANES), 1) < BRICK
    low_quarter = iota((BRICK // 2, LANES), 1) < BRICK
    sign = jnp.where(low_half, -1.0, 1.0)
    row_zero = (iota((BRICK, LANES), 0) == 0) & (iota((BRICK, LANES), 1) % BRICK == 0)

    def plane(kz):
        inner = (kz > 0) & (kz < 32)
        im_row = jnp.where(inner, 32 + kz, kz)
        re = zs[pl.ds(kz, BRICK, stride=BRICK), :]
        im = zs[pl.ds(im_row, BRICK, stride=BRICK), :]
        im = jnp.where(inner, im, 0.0)
        spec = dot(stack_lanes(jnp.concatenate([re, im], axis=1)), ty)
        spec = dot(cs, stack_rows(spec))
        s_re = spec[:BRICK, :LANES] + spec[BRICK:, LANES:]
        s_im = spec[:BRICK, LANES:] - spec[BRICK:, :LANES]
        m_re = pltpu.roll(s_re, BRICK, 1)
        m_im = pltpu.roll(s_im, BRICK, 1)
        inv = jnp.minimum(
            lax.rsqrt((s_re * s_re + s_im * s_im) * (m_re * m_re + m_im * m_im)), 1.0 / FLOOR
        )
        prod = jnp.where(low_half, s_re * m_re + s_im * m_im, s_im * m_re - s_re * m_im)
        cross = jnp.where(row_zero & (kz == 0), 0.0, prod * inv)
        back_y = dot(stack_lanes(cross), tiy)
        back_x = dot(tix, stack_rows(back_y))
        corr = back_x[:BRICK] + sign * pltpu.roll(back_x[BRICK:], BRICK, 1)
        even, odd_x = corr[: BRICK // 2], corr[BRICK // 2 :]
        qs[pl.ds(kz, BRICK // 2, stride=BRICK), :] = jnp.where(
            low_quarter, even, pltpu.roll(odd_x, BRICK, 1)
        )

        @pl.when(inner)
        def _():
            qs[pl.ds(im_row, BRICK // 2, stride=BRICK), :] = jnp.where(
                low_quarter, pltpu.roll(even, BRICK, 1), odd_x
            )

    def planes(i, carry):
        for k in range(3):
            plane(3 * i + k)
        return carry

    lax.fori_loop(0, 11, planes, 0)

    def last(i, carry):
        start = pl.multiple_of(2 * i * BRICK, BRICK)
        data = jnp.concatenate([qs[pl.ds(start, BRICK), :], qs[pl.ds(start + BRICK, BRICK), :]], axis=1)
        out_ref[:, pl.ds(pl.multiple_of(2 * i * LANES, LANES), 2 * LANES)] = dot(tiz, stack_rows(data))
        return carry

    lax.fori_loop(0, BRICK // 4, last, 0)


def halves(table):
    high = table.astype(ml_dtypes.bfloat16)
    low = (table - high.astype(np.float64)).astype(ml_dtypes.bfloat16)
    return high, low


@functools.cache
def tables():
    wave = np.arange(BRICK)
    angle = 2.0 * np.pi / BRICK * (wave[:, None] * wave[None, :] % BRICK)
    cos, sin = np.cos(angle) / 8.0, np.sin(angle) / 8.0
    high, low = halves(np.concatenate([cos[:33], -sin[1:32]], axis=0))
    fz = np.concatenate([high, high, low], axis=1)
    eye = np.eye(2)
    cos2, sin2 = np.kron(eye, cos), np.kron(eye, sin)
    high, low = halves(np.block([[cos2, -sin2], [sin2, cos2]]))
    ty = np.concatenate([high, high, low], axis=0)
    high, low = halves(np.concatenate([cos, sin], axis=0))
    cs = np.concatenate([high, high, low], axis=1)
    return fz, ty, cs


def compute(shifts, raw, par):
    vmem = pl.BlockSpec(memory_space=pltpu.VMEM)
    return pl.pallas_call(
        compute_kernel,
        out_shape=jax.ShapeDtypeStruct((BRICK // 2, BRICK * BRICK), F32),
        in_specs=[pl.BlockSpec(memory_space=pltpu.SMEM)] + [vmem] * 5,
        out_specs=vmem,
        scratch_shapes=[
            pltpu.VMEM((8 * COLS_R, LANES), F32),
            pltpu.VMEM((16, COLS_R * LANES), BF16),
            pltpu.VMEM((16, COLS_R * LANES), BF16),
            pltpu.VMEM((BRICK, COLS_V * LANES), F32),
            pltpu.VMEM((8, COLS_U * LANES), F32),
            pltpu.VMEM((16, COLS_U * LANES), BF16),
            pltpu.VMEM((16, COLS_U * LANES), BF16),
            pltpu.VMEM((BRICK * BRICK, LANES), F32),
            pltpu.VMEM((BRICK * BRICK // 2, LANES), F32),
        ],
        compiler_params=pltpu.CompilerParams(vmem_limit_bytes=40 * 1024 * 1024),
    )(shifts, raw, par, *[jnp.asarray(table) for table in tables()])


def per_device(images, offsets, fractions, shifts):
    raw, par = exchange(images, offsets, fractions)
    return compute(shifts, raw, par)[None]


def solution(mesh):
    placed = (
        P("exp", None, "tile", None),
        P(None, "depth"),
        P(None, "depth"),
        P(("tile", "depth"), None),
    )
    return jax.shard_map(
        per_device,
        mesh=mesh,
        in_specs=placed,
        out_specs=P(("tile", "depth"), "exp", None),
        check_vma=False,
    )
```

```python
import functools
import math

import jax
import jax.numpy as jnp
import ml_dtypes
import numpy as np
from jax import lax
from jax.experimental import pallas as pl
from jax.experimental.pallas import tpu as pltpu
from jax.sharding import PartitionSpec as P

MESH = pl.DeviceIdType.MESH
BRICK = 64
LANES = 128
EDGE = 24
COLS_R = BRICK + 2 * EDGE
COLS_V = BRICK + 32
COLS_U = BRICK + 16
MAIN = BRICK + EDGE
PEERS = 16
FLOOR = 0.01
UN2, UN3, UN4, PB = 48, 32, 16, 33
F32 = jnp.float32
BF16 = jnp.bfloat16


def exchange_kernel(off_ref, frac_ref, img_ref, raw_ref, par_ref, tile_ref, par_send, par_recv, send, recv, local):
    e = lax.axis_index("exp")
    t = lax.axis_index("tile")
    d = lax.axis_index("depth")
    tiles = lax.axis_size("tile")
    other = 1 - e
    half = d // 8
    d_far = (d // 4) * 4 + lax.rem(lax.rem(d, 4) + 3 - 2 * e, 4)
    t_to = lax.rem(t + 1 - 2 * half + tiles, tiles)
    t_from = lax.rem(t - 1 + 2 * half + tiles, tiles)

    def lanes_of(depth):
        return pl.ds(pl.multiple_of(lax.rem(depth, 8) // 2 * LANES, LANES), LANES)

    barrier = pltpu.get_barrier_semaphore()
    partners = [(e, t, lax.rem(d + k, PEERS)) for k in range(1, PEERS)]
    partners += [(other, t, d), (other, t, d_far)]
    partners += [(e, t_to, d), (other, t_to, d), (e, t_from, d), (other, t_from, d)]
    for partner in partners:
        pl.semaphore_signal(barrier, inc=1, device_id=partner, device_id_type=MESH)

    main_src = pl.ds(pl.multiple_of((BRICK - EDGE) * half, 8), MAIN)
    main_dst = pl.ds(pl.multiple_of(EDGE * (1 - half), 8), MAIN)
    strip_src = pl.ds(pl.multiple_of((2 * BRICK - EDGE) * (1 - half), 8), EDGE)
    strip_dst = pl.ds(pl.multiple_of(MAIN * half, 8), EDGE)

    own = pltpu.make_async_copy(
        img_ref.at[0, :, main_src, lanes_of(d)], raw_ref.at[e, :, main_dst, :], local.at[0]
    )
    own.start()

    row = lax.broadcasted_iota(jnp.int32, (8, LANES), 0)
    cam = lax.broadcasted_iota(jnp.int32, (8, LANES), 1) % 4
    tile = jnp.zeros((8, LANES), F32)
    for c in range(4):
        for z in range(4):
            tile = jnp.where((row == z) & (cam == c), off_ref[c, z].astype(F32), tile)
            tile = jnp.where((row == z + 4) & (cam == c), frac_ref[c, z], tile)
    tile_ref[...] = tile

    own_par = pltpu.make_async_copy(tile_ref, par_ref.at[d], local.at[1])
    own_par.start()

    pl.semaphore_wait(barrier, len(partners))

    copies = []
    for index, (target_e, target_d) in enumerate([(e, d), (other, d)]):
        copies.append(
            pltpu.make_async_remote_copy(
                src_ref=img_ref.at[0, :, strip_src, lanes_of(target_d)],
                dst_ref=raw_ref.at[e, :, strip_dst, :],
                send_sem=send.at[2 + index],
                recv_sem=recv.at[2 + index],
                device_id=(target_e, t_to, target_d),
                device_id_type=MESH,
            )
        )
    for index, target_d in enumerate([d, d_far]):
        cams = pl.ds(2 * index, 2)
        copies.append(
            pltpu.make_async_remote_copy(
                src_ref=img_ref.at[0, cams, main_src, lanes_of(target_d)],
                dst_ref=raw_ref.at[e, cams, main_dst, :],
                send_sem=send.at[index],
                recv_sem=recv.at[index],
                device_id=(other, t, target_d),
                device_id_type=MESH,
            )
        )
    for k in range(1, PEERS):
        copies.append(
            pltpu.make_async_remote_copy(
                src_ref=tile_ref,
                dst_ref=par_ref.at[d],
                send_sem=par_send.at[k],
                recv_sem=par_recv.at[k],
                device_id=(e, t, lax.rem(d + k, PEERS)),
                device_id_type=MESH,
            )
        )
    for copy in copies:
        copy.start()
    own.wait()
    own_par.wait()
    for copy in copies:
        copy.wait()


def exchange(images, offsets, fractions):
    smem = pl.BlockSpec(memory_space=pltpu.SMEM)
    anywhere = pl.BlockSpec(memory_space=pl.ANY)
    return pl.pallas_call(
        exchange_kernel,
        out_shape=[
            jax.ShapeDtypeStruct((2, 4, COLS_R, LANES), F32),
            jax.ShapeDtypeStruct((PEERS, 8, LANES), F32),
        ],
        in_specs=[smem, smem, anywhere],
        out_specs=[anywhere, anywhere],
        scratch_shapes=[
            pltpu.VMEM((8, LANES), F32),
            pltpu.SemaphoreType.DMA((PEERS,)),
            pltpu.SemaphoreType.DMA((PEERS,)),
            pltpu.SemaphoreType.DMA((4,)),
            pltpu.SemaphoreType.DMA((4,)),
            pltpu.SemaphoreType.DMA((2,)),
        ],
        compiler_params=pltpu.CompilerParams(collective_id=0, has_side_effects=True),
    )(offsets, fractions, images)


def split(value):
    high = value.astype(BF16)
    low = (value - high.astype(F32)).astype(BF16)
    return high, low


def stack_rows(value):
    high, low = split(value)
    return jnp.concatenate([high, low, high], axis=0)


def stack_lanes(value):
    high, low = split(value)
    return jnp.concatenate([high, low, high], axis=1)


def twice(value):
    high, low = split(value)
    return jnp.concatenate([high, low[:, :BRICK]], axis=1)


def dot(left, right):
    return jnp.dot(left, right, preferred_element_type=F32)


def turn_cos(turns):
    return jnp.cos((turns & (BRICK - 1)).astype(F32) * (2.0 * math.pi / BRICK)) * 0.125


def iota(shape, axis):
    return lax.broadcasted_iota(jnp.int32, shape, axis)


def compute_kernel(
    shift_ref, raw_ref, par_ref, fz_ref, ty_ref, cs_ref, out_ref, r8, rh, rl, g, a8, uh, ul, zs, qs
):
    e = lax.axis_index("exp")
    odd = lax.rem(lax.axis_index("depth"), 2)
    sz, sx, sy = shift_ref[0, 0], shift_ref[0, 1], shift_ref[0, 2]

    r = iota((2 * BRICK, LANES), 0)
    c = iota((2 * BRICK, LANES), 1)
    inv_y = turn_cos((r % BRICK) * (c % BRICK + sy) + 16 * (r // BRICK - c // BRICK))
    y_high, y_low = split(inv_y)
    tiy = jnp.concatenate([y_high, y_high, y_low], axis=0)
    x_of = 2 * (r % (BRICK // 2)) + (r % BRICK) // (BRICK // 2)
    tix = twice(turn_cos((c % BRICK) * (x_of + sx) - 16 * (r // BRICK)))
    r = iota((BRICK // 2, LANES), 0)
    c = iota((BRICK // 2, LANES), 1) % BRICK
    kz = jnp.where(c > 32, c - 32, c)
    weight = jnp.where((kz == 0) | (kz == 32), 1.0, 2.0)
    tiz = twice(weight * turn_cos(kz * (r + 32 * e + sz) + jnp.where(c > 32, 16, 0)))

    sub = iota((8, LANES), 0)
    offs, fracs = [], []
    for i in range(PEERS // 2):
        a, b = par_ref[2 * i], par_ref[2 * i + 1]
        offs.append(jnp.where(sub < 4, a, pltpu.roll(b, 4, 0)))
        fracs.append(jnp.where(sub < 4, pltpu.roll(a, 4, 0), b))
    off = jnp.concatenate(offs, axis=0)
    frac = jnp.concatenate(fracs, axis=0)
    s_of = iota((BRICK, LANES), 1) % BRICK // 4 - 7

    def tent(distance):
        return jnp.maximum(0.0, 1.0 - jnp.abs(distance - frac) / 1.5)

    total = tent(-2.0)
    for tap in range(-1, 4):
        total = total + tent(float(tap))
    weights = tent(s_of.astype(F32) - off) / total * 0.25
    back = twice(weights)
    turned = jnp.concatenate([weights, weights], axis=0).T[:BRICK] * 0.0625
    forward = twice(turned)
    ones = jnp.sum(turned[:, :BRICK], axis=1, keepdims=True)
    first = ones[0:8]
    for i in range(1, 8):
        first = first + ones[8 * i : 8 * i + 8]
    first = first + pltpu.roll(jnp.broadcast_to(first, (8, LANES)), 4, 0)
    log_first = jnp.log(first)

    low_lane = iota((COLS_R, LANES), 1) < BRICK
    pick = low_lane != (odd == 1)
    is_odd = odd == 1
    for cam in range(4):
        one, two = raw_ref[0, cam], raw_ref[1, cam]
        kept = jnp.where(is_odd, two, one)
        moved = jnp.where(is_odd, one, two)
        both = jnp.where(pick, kept, pltpu.roll(moved, BRICK, 1))
        ratio = jnp.log(both) - log_first[cam : cam + 1, :]
        r8[cam * COLS_R : (cam + 1) * COLS_R, :] = ratio
        r8[(cam + 4) * COLS_R : (cam + 5) * COLS_R, :] = pltpu.roll(ratio, COLS_R - 1, 0)

    for x in range(COLS_R - 2):
        col = jnp.concatenate(
            [r8[pl.ds(x, 8, stride=COLS_R), :], r8[pl.ds(x + 2, 8, stride=COLS_R), :]], axis=0
        )
        high, low = split(col)
        rh[:, x * LANES : (x + 1) * LANES] = high
        rl[:, x * LANES : (x + 1) * LANES] = low

    def windows(high_ref, low_ref, x):
        def of(ref):
            return [ref[:, pl.ds(pl.multiple_of((x + 1 + 4 * q) * LANES, LANES), 2 * LANES)] for q in range(4)]

        high = of(high_ref)
        return jnp.concatenate(high + of(low_ref) + high, axis=0)

    def second(i, carry):
        for k in range(UN2):
            x = 2 * (UN2 * i + k)
            volume = jnp.exp(dot(back, windows(rh, rl, x)))
            g[:, pl.ds(pl.multiple_of(x * LANES, LANES), 2 * LANES)] = dot(forward, stack_rows(volume))
        return carry

    lax.fori_loop(0, COLS_V // 2 // UN2, second, 0)

    chunk = 8
    for u in range(0, COLS_U, chunk):
        n = (chunk + 1) * LANES

        def group(row, shift):
            total = None
            for q in range(4):
                start = (u + shift + 12 - 4 * q) * LANES
                part = g[16 * q + row : 16 * q + row + 8, start : start + n]
                total = part if total is None else total + part
            return total

        pairs = group(0, 2) + group(8, 0)
        proj = pairs[:, LANES:] + pltpu.roll(pairs[:, : chunk * LANES], 4, 0)
        log_proj = jnp.log(proj)
        for i in range(chunk):
            ratio = r8[pl.ds(u + i + 16, 8, stride=COLS_R), :]
            a8[:, (u + i) * LANES : (u + i + 1) * LANES] = (
                2.0 * ratio + log_first - log_proj[:, i * LANES : (i + 1) * LANES]
            )

    def column(u):
        return a8[:, u * LANES : (u + 1) * LANES]

    def pair(u):
        return jnp.where(sub < 4, column(u), pltpu.roll(column(u + 1), 4, 0))

    for u in range(COLS_U - 3):
        high, low = split(jnp.concatenate([pair(u), pair(u + 2)], axis=0))
        uh[:, u * LANES : (u + 1) * LANES] = high
        ul[:, u * LANES : (u + 1) * LANES] = low

    fz = fz_ref[...]

    def third(i, carry):
        for k in range(UN3):
            x = 2 * (UN3 * i + k)
            volume = jnp.exp(dot(back, windows(uh, ul, x)))
            spec = dot(fz, stack_rows(volume))
            start = pl.multiple_of(x * BRICK, BRICK)
            zs[pl.ds(start, BRICK), :] = spec[:, :LANES]
            zs[pl.ds(start + BRICK, BRICK), :] = spec[:, LANES:]
        return carry

    lax.fori_loop(0, BRICK // 2 // UN3, third, 0)

    ty = ty_ref[...]
    cs = cs_ref[...]
    low_half = iota((BRICK, LANES), 1) < BRICK
    low_quarter = iota((BRICK // 2, LANES), 1) < BRICK
    sign = jnp.where(low_half, -1.0, 1.0)
    row_zero = (iota((BRICK, LANES), 0) == 0) & (iota((BRICK, LANES), 1) % BRICK == 0)

    def load_plane(kz):
        inner = (kz > 0) & (kz < 32)
        re = zs[pl.ds(kz, BRICK, stride=BRICK), :]
        im = zs[pl.ds(jnp.where(inner, 32 + kz, kz), BRICK, stride=BRICK), :]
        return jnp.concatenate([re, jnp.where(inner, im, 0.0)], axis=1)

    def cross_of(spec, kz):
        spec = dot(cs, stack_rows(spec))
        s_re = spec[:BRICK, :LANES] + spec[BRICK:, LANES:]
        s_im = spec[:BRICK, LANES:] - spec[BRICK:, :LANES]
        m_re = pltpu.roll(s_re, BRICK, 1)
        m_im = pltpu.roll(s_im, BRICK, 1)
        inv = jnp.minimum(
            lax.rsqrt((s_re * s_re + s_im * s_im) * (m_re * m_re + m_im * m_im)), 1.0 / FLOOR
        )
        prod = jnp.where(low_half, s_re * m_re + s_im * m_im, s_im * m_re - s_re * m_im)
        return jnp.where(row_zero & (kz == 0), 0.0, prod * inv)

    def store_plane(back_y, kz):
        inner = (kz > 0) & (kz < 32)
        back_x = dot(tix, stack_rows(back_y))
        corr = back_x[:BRICK] + sign * pltpu.roll(back_x[BRICK:], BRICK, 1)
        even, odd_x = corr[: BRICK // 2], corr[BRICK // 2 :]
        qs[pl.ds(kz, BRICK // 2, stride=BRICK), :] = jnp.where(
            low_quarter, even, pltpu.roll(odd_x, BRICK, 1)
        )
        im_row = jnp.where(inner, 32 + kz, BRICK * BRICK // 2)
        qs[pl.ds(im_row, BRICK // 2, stride=BRICK), :] = jnp.where(
            low_quarter, pltpu.roll(even, BRICK, 1), odd_x
        )

    def planes(i, carry):
        ids = [PB * i + k for k in range(PB)]
        spec = dot(stack_lanes(jnp.concatenate([load_plane(kz) for kz in ids], axis=0)), ty)
        cross = [cross_of(spec[BRICK * k : BRICK * (k + 1)], kz) for k, kz in enumerate(ids)]
        back_y = dot(stack_lanes(jnp.concatenate(cross, axis=0)), tiy)
        for k, kz in enumerate(ids):
            store_plane(back_y[BRICK * k : BRICK * (k + 1)], kz)
        return carry

    lax.fori_loop(0, 33 // PB, planes, 0)

    def last(i, carry):
        for k in range(UN4):
            x = UN4 * i + k
            start = pl.multiple_of(2 * x * BRICK, BRICK)
            data = jnp.concatenate([qs[pl.ds(start, BRICK), :], qs[pl.ds(start + BRICK, BRICK), :]], axis=1)
            out_ref[:, pl.ds(pl.multiple_of(2 * x * LANES, LANES), 2 * LANES)] = dot(tiz, stack_rows(data))
        return carry

    lax.fori_loop(0, BRICK // 4 // UN4, last, 0)


def halves(table):
    high = table.astype(ml_dtypes.bfloat16)
    low = (table - high.astype(np.float64)).astype(ml_dtypes.bfloat16)
    return high, low


@functools.cache
def tables():
    wave = np.arange(BRICK)
    angle = 2.0 * np.pi / BRICK * (wave[:, None] * wave[None, :] % BRICK)
    cos, sin = np.cos(angle) / 8.0, np.sin(angle) / 8.0
    high, low = halves(np.concatenate([cos[:33], -sin[1:32]], axis=0))
    fz = np.concatenate([high, high, low], axis=1)
    eye = np.eye(2)
    cos2, sin2 = np.kron(eye, cos), np.kron(eye, sin)
    high, low = halves(np.block([[cos2, -sin2], [sin2, cos2]]))
    ty = np.concatenate([high, high, low], axis=0)
    high, low = halves(np.concatenate([cos, sin], axis=0))
    cs = np.concatenate([high, high, low], axis=1)
    return fz, ty, cs


def compute(shifts, raw, par):
    vmem = pl.BlockSpec(memory_space=pltpu.VMEM)
    return pl.pallas_call(
        compute_kernel,
        out_shape=jax.ShapeDtypeStruct((BRICK // 2, BRICK * BRICK), F32),
        in_specs=[pl.BlockSpec(memory_space=pltpu.SMEM)] + [vmem] * 5,
        out_specs=vmem,
        scratch_shapes=[
            pltpu.VMEM((8 * COLS_R, LANES), F32),
            pltpu.VMEM((16, COLS_R * LANES), BF16),
            pltpu.VMEM((16, COLS_R * LANES), BF16),
            pltpu.VMEM((BRICK, COLS_V * LANES), F32),
            pltpu.VMEM((8, COLS_U * LANES), F32),
            pltpu.VMEM((16, COLS_U * LANES), BF16),
            pltpu.VMEM((16, COLS_U * LANES), BF16),
            pltpu.VMEM((BRICK * BRICK, LANES), F32),
            pltpu.VMEM((BRICK * BRICK, LANES), F32),
        ],
        compiler_params=pltpu.CompilerParams(vmem_limit_bytes=40 * 1024 * 1024),
    )(shifts, raw, par, *[jnp.asarray(table) for table in tables()])


def per_device(images, offsets, fractions, shifts):
    raw, par = exchange(images, offsets, fractions)
    return compute(shifts, raw, par)[None]


def solution(mesh):
    placed = (
        P("exp", None, "tile", None),
        P(None, "depth"),
        P(None, "depth"),
        P(("tile", "depth"), None),
    )
    return jax.shard_map(
        per_device,
        mesh=mesh,
        in_specs=placed,
        out_specs=P(("tile", "depth"), "exp", None),
        check_vma=False,
    )
```

```python
import functools
import math

import jax
import jax.numpy as jnp
import ml_dtypes
import numpy as np
from jax import lax
from jax.experimental import pallas as pl
from jax.experimental.pallas import tpu as pltpu
from jax.sharding import PartitionSpec as P

MESH = pl.DeviceIdType.MESH
BRICK = 64
LANES = 128
EDGE = 24
COLS_R = BRICK + 2 * EDGE
COLS_V = BRICK + 32
COLS_U = BRICK + 16
MAIN = BRICK + EDGE
PEERS = 16
FLOOR = 0.01
F32 = jnp.float32
BF16 = jnp.bfloat16
VMEM_LIMIT = 60 * 1024 * 1024
HANDED = [
    ((PEERS, 8, LANES), F32),
    ((8 * COLS_R, LANES), F32),
    ((16, COLS_R * LANES), BF16),
    ((16, COLS_R * LANES), BF16),
    ((2 * BRICK, 3 * BRICK), BF16),
    ((4 * BRICK, 2 * LANES), BF16),
    ((BRICK // 2, 3 * BRICK), BF16),
]
TABLES = [((BRICK, 3 * BRICK), BF16), ((12 * BRICK, 4 * BRICK), BF16), ((2 * BRICK, 3 * BRICK), BF16)]


def split(value):
    high = value.astype(BF16)
    low = (value - high.astype(F32)).astype(BF16)
    return high, low


def stack_rows(value):
    high, low = split(value)
    return jnp.concatenate([high, low, high], axis=0)


def stack_lanes(value):
    high, low = split(value)
    return jnp.concatenate([high, low, high], axis=1)


def twice(value):
    high, low = split(value)
    return jnp.concatenate([high, low[:, :BRICK]], axis=1)


def dot(left, right):
    return jnp.dot(left, right, preferred_element_type=F32)


def turn_cos(turns):
    return jnp.cos((turns & (BRICK - 1)).astype(F32) * (2.0 * math.pi / BRICK)) * 0.125


def iota(shape, axis):
    return lax.broadcasted_iota(jnp.int32, shape, axis)


def exchange_kernel(
    off_hbm, frac_hbm, shift_hbm, img_ref, par_out, r8_out, rh_out, rl_out, tix_out, tiy_out, tiz_out,
    off_ref, frac_ref, shift_ref, stage, stage_far, own, far, packed,
    par_ref, r8, rh, rl, tix_ref, tiy_ref, tiz_ref, local, out_sem, z_send, z_recv, y_send, y_recv, i_send, i_recv,
):
    e = lax.axis_index("exp")
    t = lax.axis_index("tile")
    d = lax.axis_index("depth")
    tiles = lax.axis_size("tile")
    other = 1 - e
    yy, zh = d // 4, lax.rem(d, 4)
    half = d // 8
    side = 2 * e - 1

    def depth_of(y, z):
        return lax.rem(y, 4) * 4 + lax.rem(z + 4, 4)

    d_far = depth_of(yy, zh + side)
    t_to = lax.rem(t + 1 - 2 * half + tiles, tiles)
    t_from = lax.rem(t - 1 + 2 * half + tiles, tiles)
    z_to = [(other, t, d_far), (e, t, d_far), (other, t, depth_of(yy, zh + 2))]
    y_to = [(e, t, depth_of(yy + k, zh)) for k in range(1, 4)]
    sources = [(other, t, d_far), (e, t, depth_of(yy, zh - side)), (other, t, depth_of(yy, zh + 2))]
    sources += y_to + [(other, t, d), (e, t_from, d), (other, t_from, d)]

    barrier = pltpu.get_barrier_semaphore()
    for source in sources:
        pl.semaphore_signal(barrier, inc=1, device_id=source, device_id_type=MESH)

    def lanes_of(depth):
        return pl.ds(pl.multiple_of(lax.rem(depth, 8) // 2 * LANES, LANES), LANES)

    main_src = pl.ds(pl.multiple_of((BRICK - EDGE) * half, 8), MAIN)
    main_dst = pl.ds(pl.multiple_of(EDGE * (1 - half), 8), MAIN)
    strip_src = pl.ds(pl.multiple_of((2 * BRICK - EDGE) * (1 - half), 8), EDGE)
    strip_dst = pl.ds(pl.multiple_of(MAIN * half, 8), EDGE)

    small = [
        pltpu.make_async_copy(off_hbm, off_ref, local.at[0]),
        pltpu.make_async_copy(frac_hbm, frac_ref, local.at[1]),
        pltpu.make_async_copy(shift_hbm, shift_ref, local.at[2]),
    ]
    large = [
        pltpu.make_async_copy(img_ref.at[0, :, :, lanes_of(d)], stage, local.at[3]),
        pltpu.make_async_copy(img_ref.at[0, pl.ds(2, 2), main_src, lanes_of(d_far)], stage_far, local.at[4]),
    ]
    for copy in small + large:
        copy.start()
    small[0].wait()
    small[1].wait()

    row = iota((8, LANES), 0)
    cam = iota((8, LANES), 1) % 4
    tile = jnp.zeros((8, LANES), F32)
    for c in range(4):
        for z in range(4):
            tile = jnp.where((row == z) & (cam == c), off_ref[c, z].astype(F32), tile)
            tile = jnp.where((row == z + 4) & (cam == c), frac_ref[c, z], tile)
    par_ref[d] = tile

    def remote(source, target, sends, recvs, index, device):
        return pltpu.make_async_remote_copy(
            src_ref=source,
            dst_ref=target,
            send_sem=sends.at[index],
            recv_sem=recvs.at[index],
            device_id=device,
            device_id_type=MESH,
        )

    along_z = [remote(par_ref.at[d], par_ref.at[d], z_send, z_recv, k, to) for k, to in enumerate(z_to)]
    rows = pl.ds(pl.multiple_of(4 * yy, 4), 4)
    along_y = [remote(par_ref.at[rows], par_ref.at[rows], y_send, y_recv, k, to) for k, to in enumerate(y_to)]
    pixels = [
        remote(own.at[:, strip_src, :], packed.at[e, :, strip_dst, :], i_send, i_recv, 0, (e, t_to, d)),
        remote(own.at[:, strip_src, :], packed.at[e, :, strip_dst, :], i_send, i_recv, 1, (other, t_to, d)),
        remote(own.at[0, main_src, :], packed.at[e, 0, main_dst, :], i_send, i_recv, 2, (other, t, d)),
        remote(far, packed.at[e, 1, main_dst, :], i_send, i_recv, 3, (other, t, d_far)),
    ]

    pl.semaphore_wait(barrier, len(sources))
    for copy in along_z:
        copy.start()

    def pack(even, odd, high_half):
        low = iota(even.shape, 1) < BRICK
        kept = jnp.where(high_half, odd, even)
        moved = pltpu.roll(jnp.where(high_half, even, odd), BRICK, 1)
        return jnp.log(jnp.where(low != high_half, kept, moved))

    for copy in large:
        copy.wait()
    for pair in range(2):
        own[pair] = pack(stage[2 * pair], stage[2 * pair + 1], lax.rem(d, 2) == 1)
    far[...] = pack(stage_far[0], stage_far[1], lax.rem(d_far, 2) == 1)
    for copy in pixels:
        copy.start()
    packed[e, :, main_dst, :] = own[:, main_src, :]

    small[2].wait()
    sz, sx, sy = shift_ref[0, 0], shift_ref[0, 1], shift_ref[0, 2]
    r = iota((2 * BRICK, LANES), 0)
    c = iota((2 * BRICK, LANES), 1)
    y_high, y_low = split(turn_cos((r % BRICK) * (c % BRICK + sy) + 16 * (r // BRICK - c // BRICK)))
    zero = jnp.zeros_like(y_low)
    tiy_ref[...] = jnp.concatenate(
        [jnp.concatenate([y_high, y_low], axis=1), jnp.concatenate([y_high, zero], axis=1)], axis=0
    )
    x_of = 2 * (r % (BRICK // 2)) + (r % BRICK) // (BRICK // 2)
    tix_ref[...] = twice(turn_cos((c % BRICK) * (x_of + sx) - 16 * (r // BRICK)))
    r = iota((BRICK // 2, LANES), 0)
    c = iota((BRICK // 2, LANES), 1) % BRICK
    kz = jnp.where(c > 32, c - 32, c)
    weight = jnp.where((kz == 0) | (kz == 32), 1.0, 2.0)
    tiz_ref[...] = twice(weight * turn_cos(kz * (r + 32 * e + sz) + jnp.where(c > 32, 16, 0)))

    results = [
        pltpu.make_async_copy(source, target, out_sem.at[k])
        for k, (source, target) in enumerate(
            [(tix_ref, tix_out), (tiy_ref, tiy_out), (tiz_ref, tiz_out), (r8, r8_out), (rh, rh_out), (rl, rl_out), (par_ref, par_out)]
        )
    ]
    for copy in results[:3]:
        copy.start()

    for copy in along_z:
        copy.wait_recv()
    for copy in along_y:
        copy.start()
    for copy in pixels:
        copy.wait_recv()

    low = iota((COLS_R, LANES), 1) < BRICK
    for pair in range(2):
        one, two = packed[0, pair], packed[1, pair]
        both = [
            jnp.where(low, one, pltpu.roll(two, BRICK, 1)),
            jnp.where(low, pltpu.roll(one, BRICK, 1), two),
        ]
        for k in range(2):
            c = 2 * pair + k
            r8[c * COLS_R : (c + 1) * COLS_R, :] = both[k]
            r8[(c + 4) * COLS_R : (c + 5) * COLS_R, :] = pltpu.roll(both[k], COLS_R - 1, 0)
    for x in range(COLS_R - 2):
        col = jnp.concatenate(
            [r8[pl.ds(x, 8, stride=COLS_R), :], r8[pl.ds(x + 2, 8, stride=COLS_R), :]], axis=0
        )
        high, lows = split(col)
        rh[:, x * LANES : (x + 1) * LANES] = high
        rl[:, x * LANES : (x + 1) * LANES] = lows

    for copy in results[3:6]:
        copy.start()
    for copy in along_y:
        copy.wait_recv()
    results[6].start()
    for copy in along_z + along_y + pixels:
        copy.wait_send()
    for copy in results:
        copy.wait()


def exchange(images, offsets, fractions, shifts):
    hbm = pl.BlockSpec(memory_space=pltpu.HBM)
    return pl.pallas_call(
        exchange_kernel,
        out_shape=[jax.ShapeDtypeStruct(shape, dtype) for shape, dtype in HANDED],
        in_specs=[hbm] * 4,
        out_specs=[hbm] * 7,
        scratch_shapes=[
            pltpu.SMEM((4, 4), jnp.int32),
            pltpu.SMEM((4, 4), F32),
            pltpu.SMEM((1, 3), jnp.int32),
            pltpu.VMEM((4, 2 * BRICK, LANES), F32),
            pltpu.VMEM((2, MAIN, LANES), F32),
            pltpu.VMEM((2, 2 * BRICK, LANES), F32),
            pltpu.VMEM((MAIN, LANES), F32),
            pltpu.VMEM((2, 2, COLS_R, LANES), F32),
            *[pltpu.VMEM(shape, dtype) for shape, dtype in HANDED],
            pltpu.SemaphoreType.DMA((5,)),
            pltpu.SemaphoreType.DMA((len(HANDED),)),
            pltpu.SemaphoreType.DMA((3,)),
            pltpu.SemaphoreType.DMA((3,)),
            pltpu.SemaphoreType.DMA((3,)),
            pltpu.SemaphoreType.DMA((3,)),
            pltpu.SemaphoreType.DMA((4,)),
            pltpu.SemaphoreType.DMA((4,)),
        ],
        compiler_params=pltpu.CompilerParams(
            collective_id=0, has_side_effects=True, vmem_limit_bytes=VMEM_LIMIT
        ),
    )(offsets, fractions, shifts, images)


def compute_kernel(
    *refs
):
    count = len(HANDED + TABLES)
    out_ref = refs[count]
    g, a8, uh, ul, zs, qs, result, done, loaded = refs[2 * count + 1 :]
    loads = [
        pltpu.make_async_copy(refs[k], refs[count + 1 + k], loaded.at[k]) for k in range(count)
    ]
    order = (0, 2, 3, 1, 7, 8, 9, 4, 5, 6)
    for k in order:
        loads[k].start()
    par_ref, r8, rh, rl, tix_ref, tiy_ref, tiz_ref, fz_ref, ty_ref, cs_ref = refs[count + 1 : 2 * count + 1]
    loads[0].wait()

    sub = iota((8, LANES), 0)
    offs, fracs = [], []
    for i in range(PEERS // 2):
        a, b = par_ref[2 * i], par_ref[2 * i + 1]
        offs.append(jnp.where(sub < 4, a, pltpu.roll(b, 4, 0)))
        fracs.append(jnp.where(sub < 4, pltpu.roll(a, 4, 0), b))
    off = jnp.concatenate(offs, axis=0)
    frac = jnp.concatenate(fracs, axis=0)
    s_of = iota((BRICK, LANES), 1) % BRICK // 4 - 7

    def tent(distance):
        return jnp.maximum(0.0, 1.0 - jnp.abs(distance - frac) / 1.5)

    total = tent(-2.0)
    for tap in range(-1, 4):
        total = total + tent(float(tap))
    weights = tent(s_of.astype(F32) - off) / total * 0.25
    back = twice(weights)
    turned = jnp.concatenate([weights, weights], axis=0).T[:BRICK] * 0.0625
    forward = twice(turned)
    ones = jnp.sum(turned[:, :BRICK], axis=1, keepdims=True)
    first = ones[0:8]
    for i in range(1, 8):
        first = first + ones[8 * i : 8 * i + 8]
    first = first + pltpu.roll(jnp.broadcast_to(first, (8, LANES)), 4, 0)
    log_first = jnp.log(first)
    by_lane = jnp.broadcast_to(jnp.sum(weights, axis=0, keepdims=True) * 0.0625, (8, LANES))
    for step in (4, 8, 16, 32):
        by_lane = by_lane + pltpu.roll(by_lane, step, 1)
    lift = jnp.sum(weights * jnp.log(by_lane[0:1]), axis=1, keepdims=True) * 0.5
    lift = jnp.broadcast_to(lift, (BRICK, 2 * LANES))

    for k in order[1:]:
        loads[k].wait()

    def windows(high_ref, low_ref, x):
        def of(ref):
            return [ref[:, (x + 1 + 4 * q) * LANES : (x + 3 + 4 * q) * LANES] for q in range(4)]

        high = of(high_ref)
        return jnp.concatenate(high + of(low_ref) + high, axis=0)

    for x in range(0, COLS_V, 2):
        volume = jnp.exp(dot(back, windows(rh, rl, x)) - lift)
        g[:, x * LANES : (x + 2) * LANES] = dot(forward, stack_rows(volume))

    chunk = 8
    for u in range(0, COLS_U, chunk):
        n = (chunk + 1) * LANES

        def group(row, shift):
            total = None
            for q in range(4):
                start = (u + shift + 12 - 4 * q) * LANES
                part = g[16 * q + row : 16 * q + row + 8, start : start + n]
                total = part if total is None else total + part
            return total

        pairs = group(0, 2) + group(8, 0)
        proj = pairs[:, LANES:] + pltpu.roll(pairs[:, : chunk * LANES], 4, 0)
        log_proj = jnp.log(proj)
        for i in range(chunk):
            ratio = r8[pl.ds(u + i + 16, 8, stride=COLS_R), :]
            a8[:, (u + i) * LANES : (u + i + 1) * LANES] = (
                2.0 * ratio - log_first - log_proj[:, i * LANES : (i + 1) * LANES]
            )

    def column(u):
        return a8[:, u * LANES : (u + 1) * LANES]

    def pair(u):
        return jnp.where(sub < 4, column(u), pltpu.roll(column(u + 1), 4, 0))

    for u in range(COLS_U - 3):
        high, low = split(jnp.concatenate([pair(u), pair(u + 2)], axis=0))
        uh[:, u * LANES : (u + 1) * LANES] = high
        ul[:, u * LANES : (u + 1) * LANES] = low

    fz = fz_ref[...]

    for x in range(0, BRICK, 2):
        volume = jnp.exp(dot(back, windows(uh, ul, x)))
        spec = dot(fz, stack_rows(volume))
        zs[x * BRICK : (x + 1) * BRICK, :] = spec[:, :LANES]
        zs[(x + 1) * BRICK : (x + 2) * BRICK, :] = spec[:, LANES:]

    ty = ty_ref[...]
    tix, tiy, tiz = tix_ref[...], tiy_ref[...], tiz_ref[...]
    cs = cs_ref[...]
    low_half = iota((BRICK, LANES), 1) < BRICK
    low_quarter = iota((BRICK // 2, LANES), 1) < BRICK
    sign = jnp.where(low_half, -1.0, 1.0)
    row_zero = (iota((BRICK, LANES), 0) == 0) & (iota((BRICK, LANES), 1) % BRICK == 0)

    def load_plane(kz):
        re = zs[pl.ds(kz, BRICK, stride=BRICK), :]
        if 0 < kz < 32:
            im = zs[pl.ds(32 + kz, BRICK, stride=BRICK), :]
        else:
            im = jnp.zeros_like(re)
        return jnp.concatenate([re, im], axis=1)

    def cross_of(spec, kz):
        spec = dot(cs, stack_rows(spec))
        s_re = spec[:BRICK, :LANES] + spec[BRICK:, LANES:]
        s_im = spec[:BRICK, LANES:] - spec[BRICK:, :LANES]
        m_re = pltpu.roll(s_re, BRICK, 1)
        m_im = pltpu.roll(s_im, BRICK, 1)
        inv = jnp.minimum(
            lax.rsqrt((s_re * s_re + s_im * s_im) * (m_re * m_re + m_im * m_im)), 1.0 / FLOOR
        )
        prod = jnp.where(low_half, s_re * m_re + s_im * m_im, s_im * m_re - s_re * m_im)
        cross = prod * inv
        return jnp.where(row_zero, 0.0, cross) if kz == 0 else cross

    def store_planes(back_y, ids):
        n = len(ids)
        back_x = dot(tix, stack_rows(jnp.concatenate(back_y, axis=1)))
        for k, kz in enumerate(ids):
            part = back_x[:, k * LANES : (k + 1) * LANES]
            corr = part[:BRICK] + sign * pltpu.roll(part[BRICK:], BRICK, 1)
            even, odd_x = corr[: BRICK // 2], corr[BRICK // 2 :]
            qs[pl.ds(kz, BRICK // 2, stride=BRICK), :] = jnp.where(
                low_quarter, even, pltpu.roll(odd_x, BRICK, 1)
            )
            if 0 < kz < 32:
                qs[pl.ds(32 + kz, BRICK // 2, stride=BRICK), :] = jnp.where(
                    low_quarter, pltpu.roll(even, BRICK, 1), odd_x
                )

    ids = range(BRICK // 2 + 1)
    spec = dot(stack_lanes(jnp.concatenate([load_plane(kz) for kz in ids], axis=0)), ty)
    cross = [cross_of(spec[BRICK * kz : BRICK * (kz + 1)], kz) for kz in ids]
    back_y = dot(jnp.concatenate(split(jnp.concatenate(cross, axis=0)), axis=1), tiy)
    back_y = back_y[:, :LANES] + back_y[:, LANES:]
    back_y = [back_y[BRICK * kz : BRICK * (kz + 1)] for kz in ids]
    for kz in range(0, len(ids), 2):
        store_planes(back_y[kz : kz + 2], ids[kz : kz + 2])

    copies = []
    for x in range(BRICK // 4):
        data = jnp.concatenate(
            [qs[BRICK * k : BRICK * (k + 1), :] for k in (2 * x, 2 * x + 1)], axis=1
        )
        result[:, 2 * x * LANES : 2 * (x + 1) * LANES] = dot(tiz, stack_rows(data))
        if x % 4 == 3:
            chunk = pl.ds((x // 4) * 8 * LANES, 8 * LANES)
            copies.append(pltpu.make_async_copy(result.at[:, chunk], out_ref.at[:, chunk], done.at[x // 4]))
            copies[-1].start()
    for copy in copies:
        copy.wait()


def halves(table):
    high = table.astype(ml_dtypes.bfloat16)
    low = (table - high.astype(np.float64)).astype(ml_dtypes.bfloat16)
    return high, low


@functools.cache
def tables():
    wave = np.arange(BRICK)
    angle = 2.0 * np.pi / BRICK * (wave[:, None] * wave[None, :] % BRICK)
    cos, sin = np.cos(angle) / 8.0, np.sin(angle) / 8.0
    high, low = halves(np.concatenate([cos[:33], -sin[1:32]], axis=0))
    fz = np.concatenate([high, high, low], axis=1)
    eye = np.eye(2)
    cos2, sin2 = np.kron(eye, cos), np.kron(eye, sin)
    high, low = halves(np.block([[cos2, -sin2], [sin2, cos2]]))
    ty = np.concatenate([high, high, low], axis=0)
    high, low = halves(np.concatenate([cos, sin], axis=0))
    cs = np.concatenate([high, high, low], axis=1)
    return fz, ty, cs


def compute(*exchanged):
    hbm = pl.BlockSpec(memory_space=pltpu.HBM)
    return pl.pallas_call(
        compute_kernel,
        out_shape=jax.ShapeDtypeStruct((BRICK // 2, BRICK * BRICK), F32),
        in_specs=[hbm] * len(HANDED + TABLES),
        out_specs=hbm,
        scratch_shapes=[
            *[pltpu.VMEM(shape, dtype) for shape, dtype in HANDED + TABLES],
            pltpu.VMEM((BRICK, COLS_V * LANES), F32),
            pltpu.VMEM((8, COLS_U * LANES), F32),
            pltpu.VMEM((16, COLS_U * LANES), BF16),
            pltpu.VMEM((16, COLS_U * LANES), BF16),
            pltpu.VMEM((BRICK * BRICK, LANES), F32),
            pltpu.VMEM((BRICK * BRICK // 2, LANES), F32),
            pltpu.VMEM((BRICK // 2, BRICK * BRICK), F32),
            pltpu.SemaphoreType.DMA((4,)),
            pltpu.SemaphoreType.DMA((len(HANDED + TABLES),)),
        ],
        compiler_params=pltpu.CompilerParams(vmem_limit_bytes=VMEM_LIMIT),
    )(*exchanged, *[jnp.asarray(table) for table in tables()])


def per_device(images, offsets, fractions, shifts):
    return compute(*exchange(images, offsets, fractions, shifts))[None]


def solution(mesh):
    placed = (
        P("exp", None, "tile", None),
        P(None, "depth"),
        P(None, "depth"),
        P(("tile", "depth"), None),
    )
    return jax.shard_map(
        per_device,
        mesh=mesh,
        in_specs=placed,
        out_specs=P(("tile", "depth"), "exp", None),
        check_vma=False,
    )
```

```python
import functools
import math

import jax
import jax.numpy as jnp
import ml_dtypes
import numpy as np
from jax import lax
from jax.experimental import pallas as pl
from jax.experimental.pallas import tpu as pltpu
from jax.sharding import PartitionSpec as P

MESH = pl.DeviceIdType.MESH
BRICK = 64
LANES = 128
EDGE = 24
COLS_R = BRICK + 2 * EDGE
COLS_V = BRICK + 32
COLS_U = BRICK + 16
MAIN = BRICK + EDGE
PEERS = 16
FLOOR = 0.01
F32 = jnp.float32
BF16 = jnp.bfloat16
VMEM_LIMIT = 60 * 1024 * 1024
HANDED = [
    ((PEERS, 8, LANES), F32),
    ((8 * COLS_R, LANES), F32),
    ((16, COLS_R * LANES), BF16),
    ((16, COLS_R * LANES), BF16),
    ((2 * BRICK, 3 * BRICK), BF16),
    ((4 * BRICK, 2 * LANES), BF16),
    ((BRICK // 2, 3 * BRICK), BF16),
]
TABLES = [((BRICK, 3 * BRICK), BF16), ((12 * BRICK, 4 * BRICK), BF16), ((2 * BRICK, 3 * BRICK), BF16)]


def split(value):
    high = value.astype(BF16)
    low = (value - high.astype(F32)).astype(BF16)
    return high, low


def stack_rows(value):
    high, low = split(value)
    return jnp.concatenate([high, low, high], axis=0)


def stack_lanes(value):
    high, low = split(value)
    return jnp.concatenate([high, low, high], axis=1)


def twice(value):
    high, low = split(value)
    return jnp.concatenate([high, low[:, :BRICK]], axis=1)


def dot(left, right):
    return jnp.dot(left, right, preferred_element_type=F32)


def turn_cos(turns):
    return jnp.cos((turns & (BRICK - 1)).astype(F32) * (2.0 * math.pi / BRICK)) * 0.125


def iota(shape, axis):
    return lax.broadcasted_iota(jnp.int32, shape, axis)


def exchange_kernel(
    off_hbm, frac_hbm, shift_hbm, img_ref, par_out, r8_out, rh_out, rl_out, tix_out, tiy_out, tiz_out,
    off_ref, frac_ref, shift_ref, stage, stage_far, own, far, packed,
    par_ref, r8, rh, rl, tix_ref, tiy_ref, tiz_ref, local, out_sem, p_send, p_recv, i_send, i_recv,
):
    e = lax.axis_index("exp")
    t = lax.axis_index("tile")
    d = lax.axis_index("depth")
    tiles = lax.axis_size("tile")
    other = 1 - e
    yy, zh = d // 4, lax.rem(d, 4)
    half = d // 8
    side = 2 * e - 1

    def depth_of(y, z):
        return lax.rem(y, 4) * 4 + lax.rem(z + 4, 4)

    d_far = depth_of(yy, zh + side)
    t_to = lax.rem(t + 1 - 2 * half + tiles, tiles)
    t_from = lax.rem(t - 1 + 2 * half + tiles, tiles)
    outer, inner = (other, t, d_far), (other, t, d)
    y_next, y_back = (e, t, depth_of(yy + 1, zh)), (e, t, depth_of(yy + 3, zh))
    sources = [outer, inner, y_next, y_back, (e, t_from, d), (other, t_from, d)]

    barrier = pltpu.get_barrier_semaphore()
    for source in sources:
        pl.semaphore_signal(barrier, inc=1, device_id=source, device_id_type=MESH)

    def lanes_of(depth):
        return pl.ds(pl.multiple_of(lax.rem(depth, 8) // 2 * LANES, LANES), LANES)

    main_src = pl.ds(pl.multiple_of((BRICK - EDGE) * half, 8), MAIN)
    main_dst = pl.ds(pl.multiple_of(EDGE * (1 - half), 8), MAIN)
    strip_src = pl.ds(pl.multiple_of((2 * BRICK - EDGE) * (1 - half), 8), EDGE)
    strip_dst = pl.ds(pl.multiple_of(MAIN * half, 8), EDGE)

    small = [
        pltpu.make_async_copy(off_hbm, off_ref, local.at[0]),
        pltpu.make_async_copy(frac_hbm, frac_ref, local.at[1]),
        pltpu.make_async_copy(shift_hbm, shift_ref, local.at[2]),
    ]
    large = [
        pltpu.make_async_copy(img_ref.at[0, :, :, lanes_of(d)], stage, local.at[3]),
        pltpu.make_async_copy(img_ref.at[0, pl.ds(2, 2), main_src, lanes_of(d_far)], stage_far, local.at[4]),
    ]
    for copy in small + large:
        copy.start()
    small[0].wait()
    small[1].wait()

    row = iota((8, LANES), 0)
    cam = iota((8, LANES), 1) % 4
    tile = jnp.zeros((8, LANES), F32)
    for c in range(4):
        for z in range(4):
            tile = jnp.where((row == z) & (cam == c), off_ref[c, z].astype(F32), tile)
            tile = jnp.where((row == z + 4) & (cam == c), frac_ref[c, z], tile)
    par_ref[d] = tile

    def remote(source, target, sends, recvs, index, device):
        return pltpu.make_async_remote_copy(
            src_ref=source,
            dst_ref=target,
            send_sem=sends.at[index],
            recv_sem=recvs.at[index],
            device_id=device,
            device_id_type=MESH,
        )

    def slabs(first, count):
        return par_ref.at[pl.ds(first, count)]

    def pass_on(first, count, index, device):
        return remote(slabs(first, count), slabs(first, count), p_send, p_recv, index, device)

    d_near = depth_of(yy, zh - side)
    own_out = pass_on(d, 1, 0, outer)
    far_in = pass_on(d_far, 1, 1, inner)
    near_out = pass_on(d_near, 1, 2, outer)
    row_next = pass_on(pl.multiple_of(4 * yy, 4), 4, 3, y_next)
    row_back = pass_on(pl.multiple_of(4 * yy, 4), 4, 4, y_back)
    row_on = pass_on(pl.multiple_of(depth_of(yy + 3, 0), 4), 4, 5, y_next)
    offers = [own_out, far_in, near_out, row_next, row_back, row_on]
    pixels = [
        remote(own.at[:, strip_src, :], packed.at[e, :, strip_dst, :], i_send, i_recv, 0, (e, t_to, d)),
        remote(own.at[:, strip_src, :], packed.at[e, :, strip_dst, :], i_send, i_recv, 1, (other, t_to, d)),
        remote(own.at[0, main_src, :], packed.at[e, 0, main_dst, :], i_send, i_recv, 2, (other, t, d)),
        remote(far, packed.at[e, 1, main_dst, :], i_send, i_recv, 3, (other, t, d_far)),
    ]

    pl.semaphore_wait(barrier, len(sources))
    own_out.start()

    def pack(even, odd, high_half):
        low = iota(even.shape, 1) < BRICK
        kept = jnp.where(high_half, odd, even)
        moved = pltpu.roll(jnp.where(high_half, even, odd), BRICK, 1)
        return jnp.log(jnp.where(low != high_half, kept, moved))

    for copy in large:
        copy.wait()
    for pair in range(2):
        own[pair] = pack(stage[2 * pair], stage[2 * pair + 1], lax.rem(d, 2) == 1)
    far[...] = pack(stage_far[0], stage_far[1], lax.rem(d_far, 2) == 1)
    for copy in pixels:
        copy.start()
    own_out.wait_recv()
    far_in.start()
    packed[e, :, main_dst, :] = own[:, main_src, :]

    small[2].wait()
    sz, sx, sy = shift_ref[0, 0], shift_ref[0, 1], shift_ref[0, 2]
    r = iota((2 * BRICK, LANES), 0)
    c = iota((2 * BRICK, LANES), 1)
    y_high, y_low = split(turn_cos((r % BRICK) * (c % BRICK + sy) + 16 * (r // BRICK - c // BRICK)))
    zero = jnp.zeros_like(y_low)
    tiy_ref[...] = jnp.concatenate(
        [jnp.concatenate([y_high, y_low], axis=1), jnp.concatenate([y_high, zero], axis=1)], axis=0
    )
    x_of = 2 * (r % (BRICK // 2)) + (r % BRICK) // (BRICK // 2)
    tix_ref[...] = twice(turn_cos((c % BRICK) * (x_of + sx) - 16 * (r // BRICK)))
    r = iota((BRICK // 2, LANES), 0)
    c = iota((BRICK // 2, LANES), 1) % BRICK
    kz = jnp.where(c > 32, c - 32, c)
    weight = jnp.where((kz == 0) | (kz == 32), 1.0, 2.0)
    tiz_ref[...] = twice(weight * turn_cos(kz * (r + 32 * e + sz) + jnp.where(c > 32, 16, 0)))

    results = [
        pltpu.make_async_copy(source, target, out_sem.at[k])
        for k, (source, target) in enumerate(
            [(tix_ref, tix_out), (tiy_ref, tiy_out), (tiz_ref, tiz_out), (r8, r8_out), (rh, rh_out), (rl, rl_out), (par_ref, par_out)]
        )
    ]
    for copy in results[:3]:
        copy.start()

    far_in.wait_recv()
    near_out.start()
    for copy in pixels:
        copy.wait_recv()

    low = iota((COLS_R, LANES), 1) < BRICK
    for pair in range(2):
        one, two = packed[0, pair], packed[1, pair]
        both = [
            jnp.where(low, one, pltpu.roll(two, BRICK, 1)),
            jnp.where(low, pltpu.roll(one, BRICK, 1), two),
        ]
        for k in range(2):
            c = 2 * pair + k
            r8[c * COLS_R : (c + 1) * COLS_R, :] = both[k]
            r8[(c + 4) * COLS_R : (c + 5) * COLS_R, :] = pltpu.roll(both[k], COLS_R - 1, 0)
    for x in range(COLS_R - 2):
        col = jnp.concatenate(
            [r8[pl.ds(x, 8, stride=COLS_R), :], r8[pl.ds(x + 2, 8, stride=COLS_R), :]], axis=0
        )
        high, lows = split(col)
        rh[:, x * LANES : (x + 1) * LANES] = high
        rl[:, x * LANES : (x + 1) * LANES] = lows

    near_out.wait_recv()
    row_next.start()
    row_back.start()
    for copy in results[3:6]:
        copy.start()
    row_next.wait_recv()
    row_on.start()
    row_back.wait_recv()
    row_on.wait_recv()
    results[6].start()
    for copy in offers + pixels:
        copy.wait_send()
    for copy in results:
        copy.wait()


def exchange(images, offsets, fractions, shifts):
    hbm = pl.BlockSpec(memory_space=pltpu.HBM)
    return pl.pallas_call(
        exchange_kernel,
        out_shape=[jax.ShapeDtypeStruct(shape, dtype) for shape, dtype in HANDED],
        in_specs=[hbm] * 4,
        out_specs=[hbm] * 7,
        scratch_shapes=[
            pltpu.SMEM((4, 4), jnp.int32),
            pltpu.SMEM((4, 4), F32),
            pltpu.SMEM((1, 3), jnp.int32),
            pltpu.VMEM((4, 2 * BRICK, LANES), F32),
            pltpu.VMEM((2, MAIN, LANES), F32),
            pltpu.VMEM((2, 2 * BRICK, LANES), F32),
            pltpu.VMEM((MAIN, LANES), F32),
            pltpu.VMEM((2, 2, COLS_R, LANES), F32),
            *[pltpu.VMEM(shape, dtype) for shape, dtype in HANDED],
            pltpu.SemaphoreType.DMA((5,)),
            pltpu.SemaphoreType.DMA((len(HANDED),)),
            pltpu.SemaphoreType.DMA((6,)),
            pltpu.SemaphoreType.DMA((6,)),
            pltpu.SemaphoreType.DMA((4,)),
            pltpu.SemaphoreType.DMA((4,)),
        ],
        compiler_params=pltpu.CompilerParams(
            collective_id=0, has_side_effects=True, vmem_limit_bytes=VMEM_LIMIT
        ),
    )(offsets, fractions, shifts, images)


def compute_kernel(
    *refs
):
    count = len(HANDED + TABLES)
    out_ref = refs[count]
    g, a8, uh, ul, zs, qs, result, done, loaded = refs[2 * count + 1 :]
    loads = [
        pltpu.make_async_copy(refs[k], refs[count + 1 + k], loaded.at[k]) for k in range(count)
    ]
    order = (0, 2, 3, 1, 7, 8, 9, 4, 5, 6)
    for k in order:
        loads[k].start()
    par_ref, r8, rh, rl, tix_ref, tiy_ref, tiz_ref, fz_ref, ty_ref, cs_ref = refs[count + 1 : 2 * count + 1]
    loads[0].wait()

    sub = iota((8, LANES), 0)
    offs, fracs = [], []
    for i in range(PEERS // 2):
        a, b = par_ref[2 * i], par_ref[2 * i + 1]
        offs.append(jnp.where(sub < 4, a, pltpu.roll(b, 4, 0)))
        fracs.append(jnp.where(sub < 4, pltpu.roll(a, 4, 0), b))
    off = jnp.concatenate(offs, axis=0)
    frac = jnp.concatenate(fracs, axis=0)
    s_of = iota((BRICK, LANES), 1) % BRICK // 4 - 7

    def tent(distance):
        return jnp.maximum(0.0, 1.0 - jnp.abs(distance - frac) / 1.5)

    total = tent(-2.0)
    for tap in range(-1, 4):
        total = total + tent(float(tap))
    weights = tent(s_of.astype(F32) - off) / total * 0.25
    back = twice(weights)
    turned = jnp.concatenate([weights, weights], axis=0).T[:BRICK] * 0.0625
    forward = twice(turned)
    ones = jnp.sum(turned[:, :BRICK], axis=1, keepdims=True)
    first = ones[0:8]
    for i in range(1, 8):
        first = first + ones[8 * i : 8 * i + 8]
    first = first + pltpu.roll(jnp.broadcast_to(first, (8, LANES)), 4, 0)
    log_first = jnp.log(first)
    by_lane = jnp.broadcast_to(jnp.sum(weights, axis=0, keepdims=True) * 0.0625, (8, LANES))
    for step in (4, 8, 16, 32):
        by_lane = by_lane + pltpu.roll(by_lane, step, 1)
    lift = jnp.sum(weights * jnp.log(by_lane[0:1]), axis=1, keepdims=True) * 0.5
    lift = jnp.broadcast_to(lift, (BRICK, 2 * LANES))

    for k in order[1:]:
        loads[k].wait()

    def windows(high_ref, low_ref, x):
        def of(ref):
            return [ref[:, (x + 1 + 4 * q) * LANES : (x + 3 + 4 * q) * LANES] for q in range(4)]

        high = of(high_ref)
        return jnp.concatenate(high + of(low_ref) + high, axis=0)

    for x in range(0, COLS_V, 2):
        volume = jnp.exp(dot(back, windows(rh, rl, x)) - lift)
        g[:, x * LANES : (x + 2) * LANES] = dot(forward, stack_rows(volume))

    chunk = 8
    for u in range(0, COLS_U, chunk):
        n = (chunk + 1) * LANES

        def group(row, shift):
            total = None
            for q in range(4):
                start = (u + shift + 12 - 4 * q) * LANES
                part = g[16 * q + row : 16 * q + row + 8, start : start + n]
                total = part if total is None else total + part
            return total

        pairs = group(0, 2) + group(8, 0)
        proj = pairs[:, LANES:] + pltpu.roll(pairs[:, : chunk * LANES], 4, 0)
        log_proj = jnp.log(proj)
        for i in range(chunk):
            ratio = r8[pl.ds(u + i + 16, 8, stride=COLS_R), :]
            a8[:, (u + i) * LANES : (u + i + 1) * LANES] = (
                2.0 * ratio - log_first - log_proj[:, i * LANES : (i + 1) * LANES]
            )

    def column(u):
        return a8[:, u * LANES : (u + 1) * LANES]

    def pair(u):
        return jnp.where(sub < 4, column(u), pltpu.roll(column(u + 1), 4, 0))

    for u in range(COLS_U - 3):
        high, low = split(jnp.concatenate([pair(u), pair(u + 2)], axis=0))
        uh[:, u * LANES : (u + 1) * LANES] = high
        ul[:, u * LANES : (u + 1) * LANES] = low

    fz = fz_ref[...]

    for x in range(0, BRICK, 2):
        volume = jnp.exp(dot(back, windows(uh, ul, x)))
        spec = dot(fz, stack_rows(volume))
        zs[x * BRICK : (x + 1) * BRICK, :] = spec[:, :LANES]
        zs[(x + 1) * BRICK : (x + 2) * BRICK, :] = spec[:, LANES:]

    ty = ty_ref[...]
    tix, tiy, tiz = tix_ref[...], tiy_ref[...], tiz_ref[...]
    cs = cs_ref[...]
    low_half = iota((BRICK, LANES), 1) < BRICK
    low_quarter = iota((BRICK // 2, LANES), 1) < BRICK
    sign = jnp.where(low_half, -1.0, 1.0)
    row_zero = (iota((BRICK, LANES), 0) == 0) & (iota((BRICK, LANES), 1) % BRICK == 0)

    def load_plane(kz):
        re = zs[pl.ds(kz, BRICK, stride=BRICK), :]
        if 0 < kz < 32:
            im = zs[pl.ds(32 + kz, BRICK, stride=BRICK), :]
        else:
            im = jnp.zeros_like(re)
        return jnp.concatenate([re, im], axis=1)

    def cross_of(spec, kz):
        spec = dot(cs, stack_rows(spec))
        s_re = spec[:BRICK, :LANES] + spec[BRICK:, LANES:]
        s_im = spec[:BRICK, LANES:] - spec[BRICK:, :LANES]
        m_re = pltpu.roll(s_re, BRICK, 1)
        m_im = pltpu.roll(s_im, BRICK, 1)
        inv = jnp.minimum(
            lax.rsqrt((s_re * s_re + s_im * s_im) * (m_re * m_re + m_im * m_im)), 1.0 / FLOOR
        )
        prod = jnp.where(low_half, s_re * m_re + s_im * m_im, s_im * m_re - s_re * m_im)
        cross = prod * inv
        return jnp.where(row_zero, 0.0, cross) if kz == 0 else cross

    def store_planes(back_y, ids):
        n = len(ids)
        back_x = dot(tix, stack_rows(jnp.concatenate(back_y, axis=1)))
        for k, kz in enumerate(ids):
            part = back_x[:, k * LANES : (k + 1) * LANES]
            corr = part[:BRICK] + sign * pltpu.roll(part[BRICK:], BRICK, 1)
            even, odd_x = corr[: BRICK // 2], corr[BRICK // 2 :]
            qs[pl.ds(kz, BRICK // 2, stride=BRICK), :] = jnp.where(
                low_quarter, even, pltpu.roll(odd_x, BRICK, 1)
            )
            if 0 < kz < 32:
                qs[pl.ds(32 + kz, BRICK // 2, stride=BRICK), :] = jnp.where(
                    low_quarter, pltpu.roll(even, BRICK, 1), odd_x
                )

    ids = range(BRICK // 2 + 1)
    spec = dot(stack_lanes(jnp.concatenate([load_plane(kz) for kz in ids], axis=0)), ty)
    cross = [cross_of(spec[BRICK * kz : BRICK * (kz + 1)], kz) for kz in ids]
    back_y = dot(jnp.concatenate(split(jnp.concatenate(cross, axis=0)), axis=1), tiy)
    back_y = back_y[:, :LANES] + back_y[:, LANES:]
    back_y = [back_y[BRICK * kz : BRICK * (kz + 1)] for kz in ids]
    for kz in range(0, len(ids), 2):
        store_planes(back_y[kz : kz + 2], ids[kz : kz + 2])

    copies = []
    for x in range(BRICK // 4):
        data = jnp.concatenate(
            [qs[BRICK * k : BRICK * (k + 1), :] for k in (2 * x, 2 * x + 1)], axis=1
        )
        result[:, 2 * x * LANES : 2 * (x + 1) * LANES] = dot(tiz, stack_rows(data))
        if x % 4 == 3:
            chunk = pl.ds((x // 4) * 8 * LANES, 8 * LANES)
            copies.append(pltpu.make_async_copy(result.at[:, chunk], out_ref.at[:, chunk], done.at[x // 4]))
            copies[-1].start()
    for copy in copies:
        copy.wait()


def halves(table):
    high = table.astype(ml_dtypes.bfloat16)
    low = (table - high.astype(np.float64)).astype(ml_dtypes.bfloat16)
    return high, low


@functools.cache
def tables():
    wave = np.arange(BRICK)
    angle = 2.0 * np.pi / BRICK * (wave[:, None] * wave[None, :] % BRICK)
    cos, sin = np.cos(angle) / 8.0, np.sin(angle) / 8.0
    high, low = halves(np.concatenate([cos[:33], -sin[1:32]], axis=0))
    fz = np.concatenate([high, high, low], axis=1)
    eye = np.eye(2)
    cos2, sin2 = np.kron(eye, cos), np.kron(eye, sin)
    high, low = halves(np.block([[cos2, -sin2], [sin2, cos2]]))
    ty = np.concatenate([high, high, low], axis=0)
    high, low = halves(np.concatenate([cos, sin], axis=0))
    cs = np.concatenate([high, high, low], axis=1)
    return fz, ty, cs


def compute(*exchanged):
    hbm = pl.BlockSpec(memory_space=pltpu.HBM)
    return pl.pallas_call(
        compute_kernel,
        out_shape=jax.ShapeDtypeStruct((BRICK // 2, BRICK * BRICK), F32),
        in_specs=[hbm] * len(HANDED + TABLES),
        out_specs=hbm,
        scratch_shapes=[
            *[pltpu.VMEM(shape, dtype) for shape, dtype in HANDED + TABLES],
            pltpu.VMEM((BRICK, COLS_V * LANES), F32),
            pltpu.VMEM((8, COLS_U * LANES), F32),
            pltpu.VMEM((16, COLS_U * LANES), BF16),
            pltpu.VMEM((16, COLS_U * LANES), BF16),
            pltpu.VMEM((BRICK * BRICK, LANES), F32),
            pltpu.VMEM((BRICK * BRICK // 2, LANES), F32),
            pltpu.VMEM((BRICK // 2, BRICK * BRICK), F32),
            pltpu.SemaphoreType.DMA((4,)),
            pltpu.SemaphoreType.DMA((len(HANDED + TABLES),)),
        ],
        compiler_params=pltpu.CompilerParams(vmem_limit_bytes=VMEM_LIMIT),
    )(*exchanged, *[jnp.asarray(table) for table in tables()])


def per_device(images, offsets, fractions, shifts):
    return compute(*exchange(images, offsets, fractions, shifts))[None]


def solution(mesh):
    placed = (
        P("exp", None, "tile", None),
        P(None, "depth"),
        P(None, "depth"),
        P(("tile", "depth"), None),
    )
    return jax.shard_map(
        per_device,
        mesh=mesh,
        in_specs=placed,
        out_specs=P(("tile", "depth"), "exp", None),
        check_vma=False,
    )
```

```python
import functools
import math

import jax
import jax.numpy as jnp
import ml_dtypes
import numpy as np
from jax import lax
from jax.experimental import pallas as pl
from jax.experimental.pallas import tpu as pltpu
from jax.sharding import PartitionSpec as P

MESH = pl.DeviceIdType.MESH
BRICK = 64
LANES = 128
EDGE = 24
COLS_R = BRICK + 2 * EDGE
COLS_V = BRICK + 32
COLS_U = BRICK + 16
MAIN = BRICK + EDGE
PEERS = 16
FLOOR = 0.01
STEP = 72
F32 = jnp.float32
BF16 = jnp.bfloat16
VMEM_LIMIT = 60 * 1024 * 1024
HANDED = [
    ((PEERS, 8, LANES), F32),
    ((8 * COLS_R, LANES), F32),
    ((16, COLS_R * LANES), BF16),
    ((16, COLS_R * LANES), BF16),
    ((2 * BRICK, 3 * BRICK), BF16),
    ((4 * BRICK, 2 * LANES), BF16),
    ((BRICK // 2, 3 * BRICK), BF16),
]
TABLES = [((BRICK, 3 * BRICK), BF16), ((12 * BRICK, 4 * BRICK), BF16), ((2 * BRICK, 3 * BRICK), BF16)]


def split(value):
    high = value.astype(BF16)
    low = (value - high.astype(F32)).astype(BF16)
    return high, low


def stack_rows(value):
    high, low = split(value)
    return jnp.concatenate([high, low, high], axis=0)


def stack_lanes(value):
    high, low = split(value)
    return jnp.concatenate([high, low, high], axis=1)


def twice(value):
    high, low = split(value)
    return jnp.concatenate([high, low[:, :BRICK]], axis=1)


def dot(left, right):
    return jnp.dot(left, right, preferred_element_type=F32)


def turn_cos(turns):
    return jnp.cos((turns & (BRICK - 1)).astype(F32) * (2.0 * math.pi / BRICK)) * 0.125


def iota(shape, axis):
    return lax.broadcasted_iota(jnp.int32, shape, axis)


def exchange_kernel(
    off_hbm, frac_hbm, shift_hbm, img_ref, par_out, r8_out, rh_out, rl_out, tix_out, tiy_out, tiz_out,
    off_ref, frac_ref, shift_ref, stage, stage_far, own, far, packed,
    par_ref, r8, rh, rl, tix_ref, tiy_ref, tiz_ref, local, out_sem, p_send, p_recv, i_send, i_recv,
):
    e = lax.axis_index("exp")
    t = lax.axis_index("tile")
    d = lax.axis_index("depth")
    tiles = lax.axis_size("tile")
    other = 1 - e
    yy, zh = d // 4, lax.rem(d, 4)
    half = d // 8
    side = 2 * e - 1

    def depth_of(y, z):
        return lax.rem(y, 4) * 4 + lax.rem(z + 4, 4)

    d_far = depth_of(yy, zh + side)
    t_to = lax.rem(t + 1 - 2 * half + tiles, tiles)
    t_from = lax.rem(t - 1 + 2 * half + tiles, tiles)
    leads = lax.rem(t, 2) == 1
    sibling = t + 1 - 2 * lax.rem(t, 2)
    z_to = [(e, zh), (other, zh + side), (e, zh + side), (other, zh + 2)]
    z_from = [(e, zh), (other, zh + side), (e, zh - side), (other, zh + 2)]
    pairs = [(k, j) for k in range(4) for j in range(4) if k or j]
    slab_to = [(z_to[k][0], t, depth_of(yy + j, z_to[k][1])) for k, j in pairs]
    slab_from = [(z_from[k][0], t, depth_of(yy + 4 - j, z_from[k][1])) for k, j in pairs]
    images_from = [(other, t, d), (other, t, d_far), (e, t_from, d), (other, t_from, d)]

    barrier = pltpu.get_barrier_semaphore()

    def greet(devices):
        for device in devices:
            pl.semaphore_signal(barrier, inc=1, device_id=device, device_id_type=MESH)

    @pl.when(leads)
    def _():
        greet(slab_from)

    greet(images_from)

    @pl.when(jnp.logical_not(leads))
    def _():
        greet([(e, sibling, d)])

    def lanes_of(depth):
        return pl.ds(pl.multiple_of(lax.rem(depth, 8) // 2 * LANES, LANES), LANES)

    main_src = pl.ds(pl.multiple_of((BRICK - EDGE) * half, 8), MAIN)
    main_dst = pl.ds(pl.multiple_of(EDGE * (1 - half), 8), MAIN)
    strip_src = pl.ds(pl.multiple_of((2 * BRICK - EDGE) * (1 - half), 8), EDGE)
    strip_dst = pl.ds(pl.multiple_of(MAIN * half, 8), EDGE)

    small = [
        pltpu.make_async_copy(off_hbm, off_ref, local.at[0]),
        pltpu.make_async_copy(frac_hbm, frac_ref, local.at[1]),
        pltpu.make_async_copy(shift_hbm, shift_ref, local.at[2]),
    ]
    large = [
        pltpu.make_async_copy(img_ref.at[0, :, :, lanes_of(d)], stage, local.at[3]),
        pltpu.make_async_copy(img_ref.at[0, pl.ds(2, 2), main_src, lanes_of(d_far)], stage_far, local.at[4]),
    ]
    for copy in small + large:
        copy.start()
    small[0].wait()
    small[1].wait()

    row = iota((8, LANES), 0)
    cam = iota((8, LANES), 1) % 4
    tile = jnp.zeros((8, LANES), F32)
    for c in range(4):
        for z in range(4):
            tile = jnp.where((row == z) & (cam == c), off_ref[c, z].astype(F32), tile)
            tile = jnp.where((row == z + 4) & (cam == c), frac_ref[c, z], tile)
    @pl.when(leads)
    def _():
        par_ref[d] = tile

    def remote(source, target, sends, recvs, index, device):
        return pltpu.make_async_remote_copy(
            src_ref=source,
            dst_ref=target,
            send_sem=sends.at[index],
            recv_sem=recvs.at[index],
            device_id=device,
            device_id_type=MESH,
        )

    slabs = [remote(par_ref.at[d], par_ref.at[d], p_send, p_recv, k, to) for k, to in enumerate(slab_to)]
    handed = remote(par_ref, par_ref, p_send, p_recv, 15, (e, sibling, d))

    pixels = [
        remote(own.at[:, strip_src, :], packed.at[e, :, strip_dst, :], i_send, i_recv, 0, (e, t_to, d)),
        remote(own.at[:, strip_src, :], packed.at[e, :, strip_dst, :], i_send, i_recv, 1, (other, t_to, d)),
        remote(own.at[0, main_src, :], packed.at[e, 0, main_dst, :], i_send, i_recv, 2, (other, t, d)),
        remote(far, packed.at[e, 1, main_dst, :], i_send, i_recv, 3, (other, t, d_far)),
    ]

    @pl.when(leads)
    def _():
        pl.semaphore_wait(barrier, len(slab_to) + 5)
        for copy in slabs:
            copy.start()

    @pl.when(jnp.logical_not(leads))
    def _():
        pl.semaphore_wait(barrier, 4)


    def pack(even, odd, high_half):
        low = iota(even.shape, 1) < BRICK
        kept = jnp.where(high_half, odd, even)
        moved = pltpu.roll(jnp.where(high_half, even, odd), BRICK, 1)
        return jnp.log(jnp.where(low != high_half, kept, moved))

    for copy in large:
        copy.wait()
    for pair in range(2):
        own[pair] = pack(stage[2 * pair], stage[2 * pair + 1], lax.rem(d, 2) == 1)
    far[...] = pack(stage_far[0], stage_far[1], lax.rem(d_far, 2) == 1)
    for copy in pixels:
        copy.start()
    packed[e, :, main_dst, :] = own[:, main_src, :]

    small[2].wait()
    sz, sx, sy = shift_ref[0, 0], shift_ref[0, 1], shift_ref[0, 2]
    r = iota((2 * BRICK, LANES), 0)
    c = iota((2 * BRICK, LANES), 1)
    y_high, y_low = split(turn_cos((r % BRICK) * (c % BRICK + sy) + 16 * (r // BRICK - c // BRICK)))
    zero = jnp.zeros_like(y_low)
    tiy_ref[...] = jnp.concatenate(
        [jnp.concatenate([y_high, y_low], axis=1), jnp.concatenate([y_high, zero], axis=1)], axis=0
    )
    x_of = 2 * (r % (BRICK // 2)) + (r % BRICK) // (BRICK // 2)
    tix_ref[...] = twice(turn_cos((c % BRICK) * (x_of + sx) - 16 * (r // BRICK)))
    r = iota((BRICK // 2, LANES), 0)
    c = iota((BRICK // 2, LANES), 1) % BRICK
    kz = jnp.where(c > 32, c - 32, c)
    weight = jnp.where((kz == 0) | (kz == 32), 1.0, 2.0)
    tiz_ref[...] = twice(weight * turn_cos(kz * (r + 32 * e + sz) + jnp.where(c > 32, 16, 0)))

    results = [
        pltpu.make_async_copy(source, target, out_sem.at[k])
        for k, (source, target) in enumerate(
            [(tix_ref, tix_out), (tiy_ref, tiy_out), (tiz_ref, tiz_out), (r8, r8_out), (rh, rh_out), (rl, rl_out), (par_ref, par_out)]
        )
    ]
    for copy in results[:3]:
        copy.start()

    for copy in pixels:
        copy.wait_recv()

    low = iota((COLS_R, LANES), 1) < BRICK
    for pair in range(2):
        one, two = packed[0, pair], packed[1, pair]
        both = [
            jnp.where(low, one, pltpu.roll(two, BRICK, 1)),
            jnp.where(low, pltpu.roll(one, BRICK, 1), two),
        ]
        for k in range(2):
            c = 2 * pair + k
            r8[c * COLS_R : (c + 1) * COLS_R, :] = both[k]
            r8[(c + 4) * COLS_R : (c + 5) * COLS_R, :] = pltpu.roll(both[k], COLS_R - 1, 0)
    for x in range(COLS_R - 2):
        col = jnp.concatenate(
            [r8[pl.ds(x, 8, stride=COLS_R), :], r8[pl.ds(x + 2, 8, stride=COLS_R), :]], axis=0
        )
        high, lows = split(col)
        rh[:, x * LANES : (x + 1) * LANES] = high
        rl[:, x * LANES : (x + 1) * LANES] = lows

    for copy in results[3:6]:
        copy.start()
    @pl.when(leads)
    def _():
        for copy in slabs:
            copy.wait_recv()
        handed.start()

    @pl.when(jnp.logical_not(leads))
    def _():
        handed.wait_recv()

    results[6].start()

    @pl.when(leads)
    def _():
        for copy in slabs + [handed]:
            copy.wait_send()

    for copy in pixels:
        copy.wait_send()
    for copy in results:
        copy.wait()


def exchange(images, offsets, fractions, shifts):
    hbm = pl.BlockSpec(memory_space=pltpu.HBM)
    return pl.pallas_call(
        exchange_kernel,
        out_shape=[jax.ShapeDtypeStruct(shape, dtype) for shape, dtype in HANDED],
        in_specs=[hbm] * 4,
        out_specs=[hbm] * 7,
        scratch_shapes=[
            pltpu.SMEM((4, 4), jnp.int32),
            pltpu.SMEM((4, 4), F32),
            pltpu.SMEM((1, 3), jnp.int32),
            pltpu.VMEM((4, 2 * BRICK, LANES), F32),
            pltpu.VMEM((2, MAIN, LANES), F32),
            pltpu.VMEM((2, 2 * BRICK, LANES), F32),
            pltpu.VMEM((MAIN, LANES), F32),
            pltpu.VMEM((2, 2, COLS_R, LANES), F32),
            *[pltpu.VMEM(shape, dtype) for shape, dtype in HANDED],
            pltpu.SemaphoreType.DMA((5,)),
            pltpu.SemaphoreType.DMA((len(HANDED),)),
            pltpu.SemaphoreType.DMA((16,)),
            pltpu.SemaphoreType.DMA((16,)),
            pltpu.SemaphoreType.DMA((4,)),
            pltpu.SemaphoreType.DMA((4,)),
        ],
        compiler_params=pltpu.CompilerParams(
            collective_id=0, has_side_effects=True, vmem_limit_bytes=VMEM_LIMIT
        ),
    )(offsets, fractions, shifts, images)


def compute_kernel(
    *refs
):
    count = len(HANDED + TABLES)
    out_ref = refs[count]
    g, a8, uh, ul, zs, qs, result, done, loaded = refs[2 * count + 1 :]
    loads = [
        pltpu.make_async_copy(refs[k], refs[count + 1 + k], loaded.at[k]) for k in range(count)
    ]
    order = (0, 2, 3, 1, 7, 8, 9, 4, 5, 6)
    for k in order:
        loads[k].start()
    par_ref, r8, rh, rl, tix_ref, tiy_ref, tiz_ref, fz_ref, ty_ref, cs_ref = refs[count + 1 : 2 * count + 1]
    loads[0].wait()

    sub = iota((8, LANES), 0)
    offs, fracs = [], []
    for i in range(PEERS // 2):
        a, b = par_ref[2 * i], par_ref[2 * i + 1]
        offs.append(jnp.where(sub < 4, a, pltpu.roll(b, 4, 0)))
        fracs.append(jnp.where(sub < 4, pltpu.roll(a, 4, 0), b))
    off = jnp.concatenate(offs, axis=0)
    frac = jnp.concatenate(fracs, axis=0)
    s_of = iota((BRICK, LANES), 1) % BRICK // 4 - 7

    def tent(distance):
        return jnp.maximum(0.0, 1.0 - jnp.abs(distance - frac) / 1.5)

    total = tent(-2.0)
    for tap in range(-1, 4):
        total = total + tent(float(tap))
    weights = tent(s_of.astype(F32) - off) / total * 0.25
    back = twice(weights)
    turned = jnp.concatenate([weights, weights], axis=0).T[:BRICK] * 0.0625
    forward = twice(turned)
    ones = jnp.sum(turned[:, :BRICK], axis=1, keepdims=True)
    first = ones[0:8]
    for i in range(1, 8):
        first = first + ones[8 * i : 8 * i + 8]
    first = first + pltpu.roll(jnp.broadcast_to(first, (8, LANES)), 4, 0)
    log_first = jnp.log(first)
    by_lane = jnp.broadcast_to(jnp.sum(weights, axis=0, keepdims=True) * 0.0625, (8, LANES))
    for step in (4, 8, 16, 32):
        by_lane = by_lane + pltpu.roll(by_lane, step, 1)
    lift = jnp.sum(weights * jnp.log(by_lane[0:1]), axis=1, keepdims=True) * 0.5
    lift = jnp.broadcast_to(lift, (BRICK, 2 * LANES))

    for k in order[1:]:
        loads[k].wait()

    def windows(high_ref, low_ref, x):
        def of(ref):
            return [ref[:, (x + 1 + 4 * q) * LANES : (x + 3 + 4 * q) * LANES] for q in range(4)]

        high = of(high_ref)
        return jnp.concatenate(high + of(low_ref) + high, axis=0)

    for x in range(0, COLS_V, 2):
        volume = jnp.exp(dot(back, windows(rh, rl, x)) - lift)
        g[:, x * LANES : (x + 2) * LANES] = dot(forward, stack_rows(volume))

    chunk = 8
    for u in range(0, COLS_U, chunk):
        n = (chunk + 1) * LANES

        def group(row, shift):
            total = None
            for q in range(4):
                start = (u + shift + 12 - 4 * q) * LANES
                part = g[16 * q + row : 16 * q + row + 8, start : start + n]
                total = part if total is None else total + part
            return total

        pairs = group(0, 2) + group(8, 0)
        proj = pairs[:, LANES:] + pltpu.roll(pairs[:, : chunk * LANES], 4, 0)
        log_proj = jnp.log(proj)
        for i in range(chunk):
            ratio = r8[pl.ds(u + i + 16, 8, stride=COLS_R), :]
            a8[:, (u + i) * LANES : (u + i + 1) * LANES] = (
                2.0 * ratio - log_first - log_proj[:, i * LANES : (i + 1) * LANES]
            )

    def column(u):
        return a8[:, u * LANES : (u + 1) * LANES]

    def pair(u):
        return jnp.where(sub < 4, column(u), pltpu.roll(column(u + 1), 4, 0))

    for u in range(COLS_U - 3):
        high, low = split(jnp.concatenate([pair(u), pair(u + 2)], axis=0))
        uh[:, u * LANES : (u + 1) * LANES] = high
        ul[:, u * LANES : (u + 1) * LANES] = low

    fz = fz_ref[...]

    for x in range(0, BRICK, 2):
        volume = jnp.exp(dot(back, windows(uh, ul, x)))
        spec = dot(fz, stack_rows(volume))
        zs[x * STEP : x * STEP + BRICK, :] = spec[:, :LANES]
        zs[(x + 1) * STEP : (x + 1) * STEP + BRICK, :] = spec[:, LANES:]

    ty = ty_ref[...]
    tix, tiy, tiz = tix_ref[...], tiy_ref[...], tiz_ref[...]
    cs = cs_ref[...]
    low_half = iota((BRICK, LANES), 1) < BRICK
    low_quarter = iota((BRICK // 2, LANES), 1) < BRICK
    sign = jnp.where(low_half, -1.0, 1.0)
    row_zero = (iota((BRICK, LANES), 0) == 0) & (iota((BRICK, LANES), 1) % BRICK == 0)

    def load_plane(kz):
        re = zs[pl.ds(kz, BRICK, stride=STEP), :]
        if 0 < kz < 32:
            im = zs[pl.ds(32 + kz, BRICK, stride=STEP), :]
        else:
            im = jnp.zeros_like(re)
        return jnp.concatenate([re, im], axis=1)

    def cross_of(spec, kz):
        spec = dot(cs, stack_rows(spec))
        s_re = spec[:BRICK, :LANES] + spec[BRICK:, LANES:]
        s_im = spec[:BRICK, LANES:] - spec[BRICK:, :LANES]
        m_re = pltpu.roll(s_re, BRICK, 1)
        m_im = pltpu.roll(s_im, BRICK, 1)
        inv = jnp.minimum(
            lax.rsqrt((s_re * s_re + s_im * s_im) * (m_re * m_re + m_im * m_im)), 1.0 / FLOOR
        )
        prod = jnp.where(low_half, s_re * m_re + s_im * m_im, s_im * m_re - s_re * m_im)
        cross = prod * inv
        return jnp.where(row_zero, 0.0, cross) if kz == 0 else cross

    def store_planes(back_y, ids):
        n = len(ids)
        back_x = dot(tix, stack_rows(jnp.concatenate(back_y, axis=1)))
        for k, kz in enumerate(ids):
            part = back_x[:, k * LANES : (k + 1) * LANES]
            corr = part[:BRICK] + sign * pltpu.roll(part[BRICK:], BRICK, 1)
            even, odd_x = corr[: BRICK // 2], corr[BRICK // 2 :]
            qs[pl.ds(kz, BRICK // 2, stride=STEP), :] = jnp.where(
                low_quarter, even, pltpu.roll(odd_x, BRICK, 1)
            )
            if 0 < kz < 32:
                qs[pl.ds(32 + kz, BRICK // 2, stride=STEP), :] = jnp.where(
                    low_quarter, pltpu.roll(even, BRICK, 1), odd_x
                )

    ids = range(BRICK // 2 + 1)
    spec = dot(stack_lanes(jnp.concatenate([load_plane(kz) for kz in ids], axis=0)), ty)
    cross = [cross_of(spec[BRICK * kz : BRICK * (kz + 1)], kz) for kz in ids]
    back_y = dot(jnp.concatenate(split(jnp.concatenate(cross, axis=0)), axis=1), tiy)
    back_y = back_y[:, :LANES] + back_y[:, LANES:]
    back_y = [back_y[BRICK * kz : BRICK * (kz + 1)] for kz in ids]
    for kz in range(0, len(ids), 2):
        store_planes(back_y[kz : kz + 2], ids[kz : kz + 2])

    copies = []
    for x in range(BRICK // 4):
        data = jnp.concatenate(
            [qs[STEP * k : STEP * k + BRICK, :] for k in (2 * x, 2 * x + 1)], axis=1
        )
        result[:, 2 * x * LANES : 2 * (x + 1) * LANES] = dot(tiz, stack_rows(data))
        if x % 4 == 3:
            chunk = pl.ds((x // 4) * 8 * LANES, 8 * LANES)
            copies.append(pltpu.make_async_copy(result.at[:, chunk], out_ref.at[:, chunk], done.at[x // 4]))
            copies[-1].start()
    for copy in copies:
        copy.wait()


def halves(table):
    high = table.astype(ml_dtypes.bfloat16)
    low = (table - high.astype(np.float64)).astype(ml_dtypes.bfloat16)
    return high, low


@functools.cache
def tables():
    wave = np.arange(BRICK)
    angle = 2.0 * np.pi / BRICK * (wave[:, None] * wave[None, :] % BRICK)
    cos, sin = np.cos(angle) / 8.0, np.sin(angle) / 8.0
    high, low = halves(np.concatenate([cos[:33], -sin[1:32]], axis=0))
    fz = np.concatenate([high, high, low], axis=1)
    eye = np.eye(2)
    cos2, sin2 = np.kron(eye, cos), np.kron(eye, sin)
    high, low = halves(np.block([[cos2, -sin2], [sin2, cos2]]))
    ty = np.concatenate([high, high, low], axis=0)
    high, low = halves(np.concatenate([cos, sin], axis=0))
    cs = np.concatenate([high, high, low], axis=1)
    return fz, ty, cs


def compute(*exchanged):
    hbm = pl.BlockSpec(memory_space=pltpu.HBM)
    return pl.pallas_call(
        compute_kernel,
        out_shape=jax.ShapeDtypeStruct((BRICK // 2, BRICK * BRICK), F32),
        in_specs=[hbm] * len(HANDED + TABLES),
        out_specs=hbm,
        scratch_shapes=[
            *[pltpu.VMEM(shape, dtype) for shape, dtype in HANDED + TABLES],
            pltpu.VMEM((BRICK, COLS_V * LANES), F32),
            pltpu.VMEM((8, COLS_U * LANES), F32),
            pltpu.VMEM((16, COLS_U * LANES), BF16),
            pltpu.VMEM((16, COLS_U * LANES), BF16),
            pltpu.VMEM((BRICK * STEP, LANES), F32),
            pltpu.VMEM((BRICK // 2 * STEP, LANES), F32),
            pltpu.VMEM((BRICK // 2, BRICK * BRICK), F32),
            pltpu.SemaphoreType.DMA((4,)),
            pltpu.SemaphoreType.DMA((len(HANDED + TABLES),)),
        ],
        compiler_params=pltpu.CompilerParams(vmem_limit_bytes=VMEM_LIMIT),
    )(*exchanged, *[jnp.asarray(table) for table in tables()])


def per_device(images, offsets, fractions, shifts):
    return compute(*exchange(images, offsets, fractions, shifts))[None]


def solution(mesh):
    placed = (
        P("exp", None, "tile", None),
        P(None, "depth"),
        P(None, "depth"),
        P(("tile", "depth"), None),
    )
    return jax.shard_map(
        per_device,
        mesh=mesh,
        in_specs=placed,
        out_specs=P(("tile", "depth"), "exp", None),
        check_vma=False,
    )
```

```python
import functools
import math

import jax
import jax.numpy as jnp
import ml_dtypes
import numpy as np
from jax import lax
from jax.experimental import pallas as pl
from jax.experimental.pallas import tpu as pltpu
from jax.sharding import PartitionSpec as P

MESH = pl.DeviceIdType.MESH
BRICK = 64
LANES = 128
EDGE = 24
COLS_R = BRICK + 2 * EDGE
COLS_V = BRICK + 32
COLS_U = BRICK + 16
MAIN = BRICK + EDGE
PEERS = 16
FLOOR = 0.01
STEP = 72
F32 = jnp.float32
BF16 = jnp.bfloat16
VMEM_LIMIT = 60 * 1024 * 1024
HANDED = [
    ((PEERS, 8, LANES), F32),
    ((8 * COLS_R, LANES), F32),
    ((16, COLS_R * LANES), BF16),
    ((16, COLS_R * LANES), BF16),
    ((2 * BRICK, 3 * BRICK), BF16),
    ((4 * BRICK, 2 * LANES), BF16),
    ((BRICK // 2, 3 * BRICK), BF16),
]
TABLES = [((BRICK, 3 * BRICK), BF16), ((12 * BRICK, 4 * BRICK), BF16), ((2 * BRICK, 3 * BRICK), BF16)]


def split(value):
    high = value.astype(BF16)
    low = (value - high.astype(F32)).astype(BF16)
    return high, low


def stack_rows(value):
    high, low = split(value)
    return jnp.concatenate([high, low, high], axis=0)


def stack_lanes(value):
    high, low = split(value)
    return jnp.concatenate([high, low, high], axis=1)


def twice(value):
    high, low = split(value)
    return jnp.concatenate([high, low[:, :BRICK]], axis=1)


def dot(left, right):
    return jnp.dot(left, right, preferred_element_type=F32)


def turn_cos(turns):
    return jnp.cos((turns & (BRICK - 1)).astype(F32) * (2.0 * math.pi / BRICK)) * 0.125


def iota(shape, axis):
    return lax.broadcasted_iota(jnp.int32, shape, axis)


def exchange_kernel(
    off_hbm, frac_hbm, shift_hbm, img_ref, fz_hbm, ty_hbm, cs_hbm, out_ref, off_ref, frac_ref, shift_ref, stage, stage_far, own, far, packed,
    par_ref, r8, rh, rl, tix_ref, tiy_ref, tiz_ref, fz_ref, ty_ref, cs_ref,
    g, a8, uh, ul, zs, qs, result, done, local, p_send, p_recv, i_send, i_recv,
):
    e = lax.axis_index("exp")
    t = lax.axis_index("tile")
    d = lax.axis_index("depth")
    tiles = lax.axis_size("tile")
    other = 1 - e
    yy, zh = d // 4, lax.rem(d, 4)
    half = d // 8
    side = 2 * e - 1

    def depth_of(y, z):
        return lax.rem(y, 4) * 4 + lax.rem(z + 4, 4)

    d_far = depth_of(yy, zh + side)
    t_to = lax.rem(t + 1 - 2 * half + tiles, tiles)
    t_from = lax.rem(t - 1 + 2 * half + tiles, tiles)
    leads = lax.rem(t, 2) == 1
    sibling = t + 1 - 2 * lax.rem(t, 2)
    z_to = [(e, zh), (other, zh + side), (e, zh + side), (other, zh + 2)]
    z_from = [(e, zh), (other, zh + side), (e, zh - side), (other, zh + 2)]
    pairs = [(k, j) for k in range(4) for j in range(4) if k or j]
    slab_to = [(z_to[k][0], t, depth_of(yy + j, z_to[k][1])) for k, j in pairs]
    slab_from = [(z_from[k][0], t, depth_of(yy + 4 - j, z_from[k][1])) for k, j in pairs]
    images_from = [(other, t, d), (other, t, d_far), (e, t_from, d), (other, t_from, d)]

    barrier = pltpu.get_barrier_semaphore()

    def greet(devices):
        for device in devices:
            pl.semaphore_signal(barrier, inc=1, device_id=device, device_id_type=MESH)

    @pl.when(leads)
    def _():
        greet(slab_from)

    greet(images_from)

    @pl.when(jnp.logical_not(leads))
    def _():
        greet([(e, sibling, d)])

    def lanes_of(depth):
        return pl.ds(pl.multiple_of(lax.rem(depth, 8) // 2 * LANES, LANES), LANES)

    main_src = pl.ds(pl.multiple_of((BRICK - EDGE) * half, 8), MAIN)
    main_dst = pl.ds(pl.multiple_of(EDGE * (1 - half), 8), MAIN)
    strip_src = pl.ds(pl.multiple_of((2 * BRICK - EDGE) * (1 - half), 8), EDGE)
    strip_dst = pl.ds(pl.multiple_of(MAIN * half, 8), EDGE)

    small = [
        pltpu.make_async_copy(off_hbm, off_ref, local.at[0]),
        pltpu.make_async_copy(frac_hbm, frac_ref, local.at[1]),
        pltpu.make_async_copy(shift_hbm, shift_ref, local.at[2]),
    ]
    large = [
        pltpu.make_async_copy(img_ref.at[0, :, :, lanes_of(d)], stage, local.at[3]),
        pltpu.make_async_copy(img_ref.at[0, pl.ds(2, 2), main_src, lanes_of(d_far)], stage_far, local.at[4]),
    ]
    constants = [
        pltpu.make_async_copy(source, target, local.at[5 + k])
        for k, (source, target) in enumerate([(fz_hbm, fz_ref), (ty_hbm, ty_ref), (cs_hbm, cs_ref)])
    ]
    for copy in small + large + constants:
        copy.start()
    small[0].wait()
    small[1].wait()

    row = iota((8, LANES), 0)
    cam = iota((8, LANES), 1) % 4
    tile = jnp.zeros((8, LANES), F32)
    for c in range(4):
        for z in range(4):
            tile = jnp.where((row == z) & (cam == c), off_ref[c, z].astype(F32), tile)
            tile = jnp.where((row == z + 4) & (cam == c), frac_ref[c, z], tile)
    @pl.when(leads)
    def _():
        par_ref[d] = tile

    def remote(source, target, sends, recvs, index, device):
        return pltpu.make_async_remote_copy(
            src_ref=source,
            dst_ref=target,
            send_sem=sends.at[index],
            recv_sem=recvs.at[index],
            device_id=device,
            device_id_type=MESH,
        )

    slabs = [remote(par_ref.at[d], par_ref.at[d], p_send, p_recv, k, to) for k, to in enumerate(slab_to)]
    handed = remote(par_ref, par_ref, p_send, p_recv, 15, (e, sibling, d))

    pixels = [
        remote(own.at[:, strip_src, :], packed.at[e, :, strip_dst, :], i_send, i_recv, 0, (e, t_to, d)),
        remote(own.at[:, strip_src, :], packed.at[e, :, strip_dst, :], i_send, i_recv, 1, (other, t_to, d)),
        remote(own.at[0, main_src, :], packed.at[e, 0, main_dst, :], i_send, i_recv, 2, (other, t, d)),
        remote(far, packed.at[e, 1, main_dst, :], i_send, i_recv, 3, (other, t, d_far)),
    ]

    @pl.when(leads)
    def _():
        pl.semaphore_wait(barrier, len(slab_to) + 5)
        for copy in slabs:
            copy.start()

    @pl.when(jnp.logical_not(leads))
    def _():
        pl.semaphore_wait(barrier, 4)


    def pack(even, odd, high_half):
        low = iota(even.shape, 1) < BRICK
        kept = jnp.where(high_half, odd, even)
        moved = pltpu.roll(jnp.where(high_half, even, odd), BRICK, 1)
        return jnp.log(jnp.where(low != high_half, kept, moved))

    for copy in large:
        copy.wait()
    for pair in range(2):
        own[pair] = pack(stage[2 * pair], stage[2 * pair + 1], lax.rem(d, 2) == 1)
    far[...] = pack(stage_far[0], stage_far[1], lax.rem(d_far, 2) == 1)
    for copy in pixels:
        copy.start()
    packed[e, :, main_dst, :] = own[:, main_src, :]

    small[2].wait()
    sz, sx, sy = shift_ref[0, 0], shift_ref[0, 1], shift_ref[0, 2]
    r = iota((2 * BRICK, LANES), 0)
    c = iota((2 * BRICK, LANES), 1)
    y_high, y_low = split(turn_cos((r % BRICK) * (c % BRICK + sy) + 16 * (r // BRICK - c // BRICK)))
    zero = jnp.zeros_like(y_low)
    tiy_ref[...] = jnp.concatenate(
        [jnp.concatenate([y_high, y_low], axis=1), jnp.concatenate([y_high, zero], axis=1)], axis=0
    )
    x_of = 2 * (r % (BRICK // 2)) + (r % BRICK) // (BRICK // 2)
    tix_ref[...] = twice(turn_cos((c % BRICK) * (x_of + sx) - 16 * (r // BRICK)))
    r = iota((BRICK // 2, LANES), 0)
    c = iota((BRICK // 2, LANES), 1) % BRICK
    kz = jnp.where(c > 32, c - 32, c)
    weight = jnp.where((kz == 0) | (kz == 32), 1.0, 2.0)
    tiz_ref[...] = twice(weight * turn_cos(kz * (r + 32 * e + sz) + jnp.where(c > 32, 16, 0)))

    for copy in pixels:
        copy.wait_recv()

    low = iota((COLS_R, LANES), 1) < BRICK
    for pair in range(2):
        one, two = packed[0, pair], packed[1, pair]
        both = [
            jnp.where(low, one, pltpu.roll(two, BRICK, 1)),
            jnp.where(low, pltpu.roll(one, BRICK, 1), two),
        ]
        for k in range(2):
            c = 2 * pair + k
            r8[c * COLS_R : (c + 1) * COLS_R, :] = both[k]
            r8[(c + 4) * COLS_R : (c + 5) * COLS_R, :] = pltpu.roll(both[k], COLS_R - 1, 0)
    for x in range(COLS_R - 2):
        col = jnp.concatenate(
            [r8[pl.ds(x, 8, stride=COLS_R), :], r8[pl.ds(x + 2, 8, stride=COLS_R), :]], axis=0
        )
        high, lows = split(col)
        rh[:, x * LANES : (x + 1) * LANES] = high
        rl[:, x * LANES : (x + 1) * LANES] = lows

    @pl.when(leads)
    def _():
        for copy in slabs:
            copy.wait_recv()
        handed.start()

    @pl.when(jnp.logical_not(leads))
    def _():
        handed.wait_recv()

    for copy in constants:
        copy.wait()
    compute_part(
        out_ref, par_ref, r8, rh, rl, tix_ref, tiy_ref, tiz_ref, fz_ref, ty_ref, cs_ref,
        g, a8, uh, ul, zs, qs, result, done,
    )

    @pl.when(leads)
    def _():
        for copy in slabs + [handed]:
            copy.wait_send()

    for copy in pixels:
        copy.wait_send()


def compute_part(
    out_ref, par_ref, r8, rh, rl, tix_ref, tiy_ref, tiz_ref, fz_ref, ty_ref, cs_ref,
    g, a8, uh, ul, zs, qs, result, done,
):
    sub = iota((8, LANES), 0)
    offs, fracs = [], []
    for i in range(PEERS // 2):
        a, b = par_ref[2 * i], par_ref[2 * i + 1]
        offs.append(jnp.where(sub < 4, a, pltpu.roll(b, 4, 0)))
        fracs.append(jnp.where(sub < 4, pltpu.roll(a, 4, 0), b))
    off = jnp.concatenate(offs, axis=0)
    frac = jnp.concatenate(fracs, axis=0)
    s_of = iota((BRICK, LANES), 1) % BRICK // 4 - 7

    def tent(distance):
        return jnp.maximum(0.0, 1.0 - jnp.abs(distance - frac) / 1.5)

    total = tent(-2.0)
    for tap in range(-1, 4):
        total = total + tent(float(tap))
    weights = tent(s_of.astype(F32) - off) / total * 0.25
    back = twice(weights)
    turned = jnp.concatenate([weights, weights], axis=0).T[:BRICK] * 0.0625
    forward = twice(turned)
    ones = jnp.sum(turned[:, :BRICK], axis=1, keepdims=True)
    first = ones[0:8]
    for i in range(1, 8):
        first = first + ones[8 * i : 8 * i + 8]
    first = first + pltpu.roll(jnp.broadcast_to(first, (8, LANES)), 4, 0)
    log_first = jnp.log(first)
    by_lane = jnp.broadcast_to(jnp.sum(weights, axis=0, keepdims=True) * 0.0625, (8, LANES))
    for step in (4, 8, 16, 32):
        by_lane = by_lane + pltpu.roll(by_lane, step, 1)
    lift = jnp.sum(weights * jnp.log(by_lane[0:1]), axis=1, keepdims=True) * 0.5
    lift = jnp.broadcast_to(lift, (BRICK, 2 * LANES))

    def windows(high_ref, low_ref, x):
        def of(ref):
            return [ref[:, (x + 1 + 4 * q) * LANES : (x + 3 + 4 * q) * LANES] for q in range(4)]

        high = of(high_ref)
        return jnp.concatenate(high + of(low_ref) + high, axis=0)

    for x in range(0, COLS_V, 2):
        volume = jnp.exp(dot(back, windows(rh, rl, x)) - lift)
        g[:, x * LANES : (x + 2) * LANES] = dot(forward, stack_rows(volume))

    chunk = 8
    for u in range(0, COLS_U, chunk):
        n = (chunk + 1) * LANES

        def group(row, shift):
            total = None
            for q in range(4):
                start = (u + shift + 12 - 4 * q) * LANES
                part = g[16 * q + row : 16 * q + row + 8, start : start + n]
                total = part if total is None else total + part
            return total

        pairs = group(0, 2) + group(8, 0)
        proj = pairs[:, LANES:] + pltpu.roll(pairs[:, : chunk * LANES], 4, 0)
        log_proj = jnp.log(proj)
        for i in range(chunk):
            ratio = r8[pl.ds(u + i + 16, 8, stride=COLS_R), :]
            a8[:, (u + i) * LANES : (u + i + 1) * LANES] = (
                2.0 * ratio - log_first - log_proj[:, i * LANES : (i + 1) * LANES]
            )

    def column(u):
        return a8[:, u * LANES : (u + 1) * LANES]

    def pair(u):
        return jnp.where(sub < 4, column(u), pltpu.roll(column(u + 1), 4, 0))

    for u in range(COLS_U - 3):
        high, low = split(jnp.concatenate([pair(u), pair(u + 2)], axis=0))
        uh[:, u * LANES : (u + 1) * LANES] = high
        ul[:, u * LANES : (u + 1) * LANES] = low

    fz = fz_ref[...]

    for x in range(0, BRICK, 2):
        volume = jnp.exp(dot(back, windows(uh, ul, x)))
        spec = dot(fz, stack_rows(volume))
        zs[x * STEP : x * STEP + BRICK, :] = spec[:, :LANES]
        zs[(x + 1) * STEP : (x + 1) * STEP + BRICK, :] = spec[:, LANES:]

    ty = ty_ref[...]
    tix, tiy, tiz = tix_ref[...], tiy_ref[...], tiz_ref[...]
    cs = cs_ref[...]
    low_half = iota((BRICK, LANES), 1) < BRICK
    low_quarter = iota((BRICK // 2, LANES), 1) < BRICK
    sign = jnp.where(low_half, -1.0, 1.0)
    row_zero = (iota((BRICK, LANES), 0) == 0) & (iota((BRICK, LANES), 1) % BRICK == 0)

    def load_plane(kz):
        re = zs[pl.ds(kz, BRICK, stride=STEP), :]
        if 0 < kz < 32:
            im = zs[pl.ds(32 + kz, BRICK, stride=STEP), :]
        else:
            im = jnp.zeros_like(re)
        return jnp.concatenate([re, im], axis=1)

    def cross_of(spec, kz):
        spec = dot(cs, stack_rows(spec))
        s_re = spec[:BRICK, :LANES] + spec[BRICK:, LANES:]
        s_im = spec[:BRICK, LANES:] - spec[BRICK:, :LANES]
        m_re = pltpu.roll(s_re, BRICK, 1)
        m_im = pltpu.roll(s_im, BRICK, 1)
        inv = jnp.minimum(
            lax.rsqrt((s_re * s_re + s_im * s_im) * (m_re * m_re + m_im * m_im)), 1.0 / FLOOR
        )
        prod = jnp.where(low_half, s_re * m_re + s_im * m_im, s_im * m_re - s_re * m_im)
        cross = prod * inv
        return jnp.where(row_zero, 0.0, cross) if kz == 0 else cross

    def store_planes(back_y, ids):
        n = len(ids)
        back_x = dot(tix, stack_rows(jnp.concatenate(back_y, axis=1)))
        for k, kz in enumerate(ids):
            part = back_x[:, k * LANES : (k + 1) * LANES]
            corr = part[:BRICK] + sign * pltpu.roll(part[BRICK:], BRICK, 1)
            even, odd_x = corr[: BRICK // 2], corr[BRICK // 2 :]
            qs[pl.ds(kz, BRICK // 2, stride=STEP), :] = jnp.where(
                low_quarter, even, pltpu.roll(odd_x, BRICK, 1)
            )
            if 0 < kz < 32:
                qs[pl.ds(32 + kz, BRICK // 2, stride=STEP), :] = jnp.where(
                    low_quarter, pltpu.roll(even, BRICK, 1), odd_x
                )

    ids = range(BRICK // 2 + 1)
    spec = dot(stack_lanes(jnp.concatenate([load_plane(kz) for kz in ids], axis=0)), ty)
    cross = [cross_of(spec[BRICK * kz : BRICK * (kz + 1)], kz) for kz in ids]
    back_y = dot(jnp.concatenate(split(jnp.concatenate(cross, axis=0)), axis=1), tiy)
    back_y = back_y[:, :LANES] + back_y[:, LANES:]
    back_y = [back_y[BRICK * kz : BRICK * (kz + 1)] for kz in ids]
    for kz in range(0, len(ids), 2):
        store_planes(back_y[kz : kz + 2], ids[kz : kz + 2])

    copies = []
    for x in range(BRICK // 4):
        data = jnp.concatenate(
            [qs[STEP * k : STEP * k + BRICK, :] for k in (2 * x, 2 * x + 1)], axis=1
        )
        result[:, 2 * x * LANES : 2 * (x + 1) * LANES] = dot(tiz, stack_rows(data))
        if x % 4 == 3:
            chunk = pl.ds((x // 4) * 8 * LANES, 8 * LANES)
            copies.append(pltpu.make_async_copy(result.at[:, chunk], out_ref.at[:, chunk], done.at[x // 4]))
            copies[-1].start()
    for copy in copies:
        copy.wait()


def halves(table):
    high = table.astype(ml_dtypes.bfloat16)
    low = (table - high.astype(np.float64)).astype(ml_dtypes.bfloat16)
    return high, low


@functools.cache
def tables():
    wave = np.arange(BRICK)
    angle = 2.0 * np.pi / BRICK * (wave[:, None] * wave[None, :] % BRICK)
    cos, sin = np.cos(angle) / 8.0, np.sin(angle) / 8.0
    high, low = halves(np.concatenate([cos[:33], -sin[1:32]], axis=0))
    fz = np.concatenate([high, high, low], axis=1)
    eye = np.eye(2)
    cos2, sin2 = np.kron(eye, cos), np.kron(eye, sin)
    high, low = halves(np.block([[cos2, -sin2], [sin2, cos2]]))
    ty = np.concatenate([high, high, low], axis=0)
    high, low = halves(np.concatenate([cos, sin], axis=0))
    cs = np.concatenate([high, high, low], axis=1)
    return fz, ty, cs


def per_device(images, offsets, fractions, shifts):
    hbm = pl.BlockSpec(memory_space=pltpu.HBM)
    result = pl.pallas_call(
        exchange_kernel,
        out_shape=jax.ShapeDtypeStruct((BRICK // 2, BRICK * BRICK), F32),
        in_specs=[hbm] * 7,
        out_specs=hbm,
        scratch_shapes=[
            pltpu.SMEM((4, 4), jnp.int32),
            pltpu.SMEM((4, 4), F32),
            pltpu.SMEM((1, 3), jnp.int32),
            pltpu.VMEM((4, 2 * BRICK, LANES), F32),
            pltpu.VMEM((2, MAIN, LANES), F32),
            pltpu.VMEM((2, 2 * BRICK, LANES), F32),
            pltpu.VMEM((MAIN, LANES), F32),
            pltpu.VMEM((2, 2, COLS_R, LANES), F32),
            *[pltpu.VMEM(shape, dtype) for shape, dtype in HANDED + TABLES],
            pltpu.VMEM((BRICK, COLS_V * LANES), F32),
            pltpu.VMEM((8, COLS_U * LANES), F32),
            pltpu.VMEM((16, COLS_U * LANES), BF16),
            pltpu.VMEM((16, COLS_U * LANES), BF16),
            pltpu.VMEM((BRICK * STEP, LANES), F32),
            pltpu.VMEM((BRICK // 2 * STEP, LANES), F32),
            pltpu.VMEM((BRICK // 2, BRICK * BRICK), F32),
            pltpu.SemaphoreType.DMA((4,)),
            pltpu.SemaphoreType.DMA((8,)),
            pltpu.SemaphoreType.DMA((16,)),
            pltpu.SemaphoreType.DMA((16,)),
            pltpu.SemaphoreType.DMA((4,)),
            pltpu.SemaphoreType.DMA((4,)),
        ],
        compiler_params=pltpu.CompilerParams(
            collective_id=0, has_side_effects=True, vmem_limit_bytes=VMEM_LIMIT
        ),
    )(offsets, fractions, shifts, images, *[jnp.asarray(table) for table in tables()])
    return result[None]


def solution(mesh):
    placed = (
        P("exp", None, "tile", None),
        P(None, "depth"),
        P(None, "depth"),
        P(("tile", "depth"), None),
    )
    return jax.shard_map(
        per_device,
        mesh=mesh,
        in_specs=placed,
        out_specs=P(("tile", "depth"), "exp", None),
        check_vma=False,
    )
```

```python
import functools
import math

import jax
import jax.numpy as jnp
import ml_dtypes
import numpy as np
from jax import lax
from jax.experimental import pallas as pl
from jax.experimental.pallas import tpu as pltpu
from jax.sharding import PartitionSpec as P

MESH = pl.DeviceIdType.MESH
BRICK = 64
LANES = 128
EDGE = 24
COLS_R = BRICK + 2 * EDGE
COLS_V = BRICK + 32
COLS_U = BRICK + 16
MAIN = BRICK + EDGE
PEERS = 16
FLOOR = 0.01
STEP = 72
F32 = jnp.float32
BF16 = jnp.bfloat16
VMEM_LIMIT = 60 * 1024 * 1024
HANDED = [
    ((PEERS, 8, LANES), F32),
    ((8 * COLS_R, LANES), F32),
    ((16, COLS_R * LANES), BF16),
    ((16, COLS_R * LANES), BF16),
    ((2 * BRICK, 3 * BRICK), BF16),
    ((4 * BRICK, 2 * LANES), BF16),
    ((BRICK // 2, 3 * BRICK), BF16),
]
TABLES = [((BRICK, 3 * BRICK), BF16), ((12 * BRICK, 4 * BRICK), BF16), ((2 * BRICK, 3 * BRICK), BF16)]


def split(value):
    high = value.astype(BF16)
    low = (value - high.astype(F32)).astype(BF16)
    return high, low


def stack_rows(value):
    high, low = split(value)
    return jnp.concatenate([high, low, high], axis=0)


def stack_lanes(value):
    high, low = split(value)
    return jnp.concatenate([high, low, high], axis=1)


def twice(value):
    high, low = split(value)
    return jnp.concatenate([high, low[:, :BRICK]], axis=1)


def dot(left, right):
    return jnp.dot(left, right, preferred_element_type=F32)


def turn_cos(turns):
    return jnp.cos((turns & (BRICK - 1)).astype(F32) * (2.0 * math.pi / BRICK)) * 0.125


def iota(shape, axis):
    return lax.broadcasted_iota(jnp.int32, shape, axis)


def exchange_kernel(
    off_hbm, frac_hbm, shift_hbm, img_ref, fz_hbm, ty_hbm, cs_hbm, out_ref, off_ref, frac_ref, shift_ref, stage, stage_far, own, far, packed,
    par_ref, r8, rh, rl, tix_ref, tiy_ref, tiz_ref, fz_ref, ty_ref, cs_ref,
    g, a8, uh, ul, zs, qs, result, done, local, p_send, p_recv, i_send, i_recv,
):
    e = lax.axis_index("exp")
    t = lax.axis_index("tile")
    d = lax.axis_index("depth")
    tiles = lax.axis_size("tile")
    other = 1 - e
    yy, zh = d // 4, lax.rem(d, 4)
    half = d // 8
    side = 2 * e - 1

    def depth_of(y, z):
        return lax.rem(y, 4) * 4 + lax.rem(z + 4, 4)

    d_far = depth_of(yy, zh + side)
    t_to = lax.rem(t + 1 - 2 * half + tiles, tiles)
    t_from = lax.rem(t - 1 + 2 * half + tiles, tiles)
    leads = lax.rem(t, 2) == 1
    sibling = t + 1 - 2 * lax.rem(t, 2)
    z_to = [(e, zh), (other, zh + side), (e, zh + side), (other, zh + 2)]
    z_from = [(e, zh), (other, zh + side), (e, zh - side), (other, zh + 2)]
    pairs = sorted([(k, j) for k in range(4) for j in range(4) if k or j], key=lambda p: -p[0] - min(p[1], 4 - p[1]))
    slab_to = [(z_to[k][0], t, depth_of(yy + j, z_to[k][1])) for k, j in pairs]
    slab_from = [(z_from[k][0], t, depth_of(yy + 4 - j, z_from[k][1])) for k, j in pairs]
    images_from = [(other, t, d), (other, t, d_far), (e, t_from, d), (other, t_from, d)]

    barrier = pltpu.get_barrier_semaphore()

    def greet(devices):
        for device in devices:
            pl.semaphore_signal(barrier, inc=1, device_id=device, device_id_type=MESH)

    @pl.when(leads)
    def _():
        greet(slab_from)

    greet(images_from)

    @pl.when(jnp.logical_not(leads))
    def _():
        greet([(e, sibling, d)])

    def lanes_of(depth):
        return pl.ds(pl.multiple_of(lax.rem(depth, 8) // 2 * LANES, LANES), LANES)

    main_src = pl.ds(pl.multiple_of((BRICK - EDGE) * half, 8), MAIN)
    main_dst = pl.ds(pl.multiple_of(EDGE * (1 - half), 8), MAIN)
    strip_src = pl.ds(pl.multiple_of((2 * BRICK - EDGE) * (1 - half), 8), EDGE)
    strip_dst = pl.ds(pl.multiple_of(MAIN * half, 8), EDGE)

    small = [
        pltpu.make_async_copy(off_hbm, off_ref, local.at[0]),
        pltpu.make_async_copy(frac_hbm, frac_ref, local.at[1]),
        pltpu.make_async_copy(shift_hbm, shift_ref, local.at[2]),
    ]
    large = [
        pltpu.make_async_copy(img_ref.at[0, :, :, lanes_of(d)], stage, local.at[3]),
        pltpu.make_async_copy(img_ref.at[0, pl.ds(2, 2), main_src, lanes_of(d_far)], stage_far, local.at[4]),
    ]
    constants = [
        pltpu.make_async_copy(source, target, local.at[5 + k])
        for k, (source, target) in enumerate([(fz_hbm, fz_ref), (ty_hbm, ty_ref), (cs_hbm, cs_ref)])
    ]
    for copy in small + large + constants:
        copy.start()
    small[0].wait()
    small[1].wait()

    row = iota((8, LANES), 0)
    cam = iota((8, LANES), 1) % 4
    tile = jnp.zeros((8, LANES), F32)
    for c in range(4):
        for z in range(4):
            tile = jnp.where((row == z) & (cam == c), off_ref[c, z].astype(F32), tile)
            tile = jnp.where((row == z + 4) & (cam == c), frac_ref[c, z], tile)
    @pl.when(leads)
    def _():
        par_ref[d] = tile

    def remote(source, target, sends, recvs, index, device):
        return pltpu.make_async_remote_copy(
            src_ref=source,
            dst_ref=target,
            send_sem=sends.at[index],
            recv_sem=recvs.at[index],
            device_id=device,
            device_id_type=MESH,
        )

    slabs = [remote(par_ref.at[d], par_ref.at[d], p_send, p_recv, k, to) for k, to in enumerate(slab_to)]
    handed = remote(par_ref, par_ref, p_send, p_recv, 15, (e, sibling, d))

    pixels = [
        remote(own.at[:, strip_src, :], packed.at[e, :, strip_dst, :], i_send, i_recv, 0, (e, t_to, d)),
        remote(own.at[:, strip_src, :], packed.at[e, :, strip_dst, :], i_send, i_recv, 1, (other, t_to, d)),
        remote(own.at[0, main_src, :], packed.at[e, 0, main_dst, :], i_send, i_recv, 2, (other, t, d)),
        remote(far, packed.at[e, 1, main_dst, :], i_send, i_recv, 3, (other, t, d_far)),
    ]

    @pl.when(leads)
    def _():
        pl.semaphore_wait(barrier, len(slab_to) + 5)
        for copy in slabs:
            copy.start()

    @pl.when(jnp.logical_not(leads))
    def _():
        pl.semaphore_wait(barrier, 4)


    def pack(even, odd, high_half):
        low = iota(even.shape, 1) < BRICK
        kept = jnp.where(high_half, odd, even)
        moved = pltpu.roll(jnp.where(high_half, even, odd), BRICK, 1)
        return jnp.log(jnp.where(low != high_half, kept, moved))

    for copy in large:
        copy.wait()
    for pair in range(2):
        own[pair] = pack(stage[2 * pair], stage[2 * pair + 1], lax.rem(d, 2) == 1)
    far[...] = pack(stage_far[0], stage_far[1], lax.rem(d_far, 2) == 1)
    for copy in pixels:
        copy.start()
    packed[e, :, main_dst, :] = own[:, main_src, :]

    small[2].wait()
    sz, sx, sy = shift_ref[0, 0], shift_ref[0, 1], shift_ref[0, 2]
    r = iota((2 * BRICK, LANES), 0)
    c = iota((2 * BRICK, LANES), 1)
    y_high, y_low = split(turn_cos((r % BRICK) * (c % BRICK + sy) + 16 * (r // BRICK - c // BRICK)))
    zero = jnp.zeros_like(y_low)
    tiy_ref[...] = jnp.concatenate(
        [jnp.concatenate([y_high, y_low], axis=1), jnp.concatenate([y_high, zero], axis=1)], axis=0
    )
    x_of = 2 * (r % (BRICK // 2)) + (r % BRICK) // (BRICK // 2)
    tix_ref[...] = twice(turn_cos((c % BRICK) * (x_of + sx) - 16 * (r // BRICK)))
    r = iota((BRICK // 2, LANES), 0)
    c = iota((BRICK // 2, LANES), 1) % BRICK
    kz = jnp.where(c > 32, c - 32, c)
    weight = jnp.where((kz == 0) | (kz == 32), 1.0, 2.0)
    tiz_ref[...] = twice(weight * turn_cos(kz * (r + 32 * e + sz) + jnp.where(c > 32, 16, 0)))

    for copy in pixels:
        copy.wait_recv()

    low = iota((COLS_R, LANES), 1) < BRICK
    for pair in range(2):
        one, two = packed[0, pair], packed[1, pair]
        both = [
            jnp.where(low, one, pltpu.roll(two, BRICK, 1)),
            jnp.where(low, pltpu.roll(one, BRICK, 1), two),
        ]
        for k in range(2):
            c = 2 * pair + k
            r8[c * COLS_R : (c + 1) * COLS_R, :] = both[k]
            r8[(c + 4) * COLS_R : (c + 5) * COLS_R, :] = pltpu.roll(both[k], COLS_R - 1, 0)
    for x in range(COLS_R - 2):
        col = jnp.concatenate(
            [r8[pl.ds(x, 8, stride=COLS_R), :], r8[pl.ds(x + 2, 8, stride=COLS_R), :]], axis=0
        )
        high, lows = split(col)
        rh[:, x * LANES : (x + 1) * LANES] = high
        rl[:, x * LANES : (x + 1) * LANES] = lows

    @pl.when(leads)
    def _():
        for copy in slabs:
            copy.wait_recv()
        handed.start()

    @pl.when(jnp.logical_not(leads))
    def _():
        handed.wait_recv()

    for copy in constants:
        copy.wait()
    compute_part(
        out_ref, par_ref, r8, rh, rl, tix_ref, tiy_ref, tiz_ref, fz_ref, ty_ref, cs_ref,
        g, a8, uh, ul, zs, qs, result, done,
    )

    @pl.when(leads)
    def _():
        for copy in slabs + [handed]:
            copy.wait_send()

    for copy in pixels:
        copy.wait_send()


def compute_part(
    out_ref, par_ref, r8, rh, rl, tix_ref, tiy_ref, tiz_ref, fz_ref, ty_ref, cs_ref,
    g, a8, uh, ul, zs, qs, result, done,
):
    sub = iota((8, LANES), 0)
    offs, fracs = [], []
    for i in range(PEERS // 2):
        a, b = par_ref[2 * i], par_ref[2 * i + 1]
        offs.append(jnp.where(sub < 4, a, pltpu.roll(b, 4, 0)))
        fracs.append(jnp.where(sub < 4, pltpu.roll(a, 4, 0), b))
    off = jnp.concatenate(offs, axis=0)
    frac = jnp.concatenate(fracs, axis=0)
    s_of = iota((BRICK, LANES), 1) % BRICK // 4 - 7

    def tent(distance):
        return jnp.maximum(0.0, 1.0 - jnp.abs(distance - frac) / 1.5)

    total = tent(-2.0)
    for tap in range(-1, 4):
        total = total + tent(float(tap))
    weights = tent(s_of.astype(F32) - off) / total * 0.25
    back = twice(weights)
    turned = jnp.concatenate([weights, weights], axis=0).T[:BRICK] * 0.0625
    forward = twice(turned)
    ones = jnp.sum(turned[:, :BRICK], axis=1, keepdims=True)
    first = ones[0:8]
    for i in range(1, 8):
        first = first + ones[8 * i : 8 * i + 8]
    first = first + pltpu.roll(jnp.broadcast_to(first, (8, LANES)), 4, 0)
    log_first = jnp.log(first)
    by_lane = jnp.broadcast_to(jnp.sum(weights, axis=0, keepdims=True) * 0.0625, (8, LANES))
    for step in (4, 8, 16, 32):
        by_lane = by_lane + pltpu.roll(by_lane, step, 1)
    lift = jnp.sum(weights * jnp.log(by_lane[0:1]), axis=1, keepdims=True) * 0.5
    lift = jnp.broadcast_to(lift, (BRICK, 2 * LANES))

    def windows(high_ref, low_ref, x):
        def of(ref):
            return [ref[:, (x + 1 + 4 * q) * LANES : (x + 3 + 4 * q) * LANES] for q in range(4)]

        high = of(high_ref)
        return jnp.concatenate(high + of(low_ref) + high, axis=0)

    for x in range(0, COLS_V, 2):
        volume = jnp.exp(dot(back, windows(rh, rl, x)) - lift)
        g[:, x * LANES : (x + 2) * LANES] = dot(forward, stack_rows(volume))

    chunk = 8
    for u in range(0, COLS_U, chunk):
        n = (chunk + 1) * LANES

        def group(row, shift):
            total = None
            for q in range(4):
                start = (u + shift + 12 - 4 * q) * LANES
                part = g[16 * q + row : 16 * q + row + 8, start : start + n]
                total = part if total is None else total + part
            return total

        pairs = group(0, 2) + group(8, 0)
        proj = pairs[:, LANES:] + pltpu.roll(pairs[:, : chunk * LANES], 4, 0)
        log_proj = jnp.log(proj)
        for i in range(chunk):
            ratio = r8[pl.ds(u + i + 16, 8, stride=COLS_R), :]
            a8[:, (u + i) * LANES : (u + i + 1) * LANES] = (
                2.0 * ratio - log_first - log_proj[:, i * LANES : (i + 1) * LANES]
            )

    def column(u):
        return a8[:, u * LANES : (u + 1) * LANES]

    def pair(u):
        return jnp.where(sub < 4, column(u), pltpu.roll(column(u + 1), 4, 0))

    for u in range(COLS_U - 3):
        high, low = split(jnp.concatenate([pair(u), pair(u + 2)], axis=0))
        uh[:, u * LANES : (u + 1) * LANES] = high
        ul[:, u * LANES : (u + 1) * LANES] = low

    fz = fz_ref[...]

    for x in range(0, BRICK, 2):
        volume = jnp.exp(dot(back, windows(uh, ul, x)))
        spec = dot(fz, stack_rows(volume))
        zs[x * STEP : x * STEP + BRICK, :] = spec[:, :LANES]
        zs[(x + 1) * STEP : (x + 1) * STEP + BRICK, :] = spec[:, LANES:]

    ty = ty_ref[...]
    tix, tiy, tiz = tix_ref[...], tiy_ref[...], tiz_ref[...]
    cs = cs_ref[...]
    low_half = iota((BRICK, LANES), 1) < BRICK
    low_quarter = iota((BRICK // 2, LANES), 1) < BRICK
    sign = jnp.where(low_half, -1.0, 1.0)
    row_zero = (iota((BRICK, LANES), 0) == 0) & (iota((BRICK, LANES), 1) % BRICK == 0)

    def load_plane(kz):
        re = zs[pl.ds(kz, BRICK, stride=STEP), :]
        if 0 < kz < 32:
            im = zs[pl.ds(32 + kz, BRICK, stride=STEP), :]
        else:
            im = jnp.zeros_like(re)
        return jnp.concatenate([re, im], axis=1)

    def cross_of(spec, kz):
        spec = dot(cs, stack_rows(spec))
        s_re = spec[:BRICK, :LANES] + spec[BRICK:, LANES:]
        s_im = spec[:BRICK, LANES:] - spec[BRICK:, :LANES]
        m_re = pltpu.roll(s_re, BRICK, 1)
        m_im = pltpu.roll(s_im, BRICK, 1)
        inv = jnp.minimum(
            lax.rsqrt((s_re * s_re + s_im * s_im) * (m_re * m_re + m_im * m_im)), 1.0 / FLOOR
        )
        prod = jnp.where(low_half, s_re * m_re + s_im * m_im, s_im * m_re - s_re * m_im)
        cross = prod * inv
        return jnp.where(row_zero, 0.0, cross) if kz == 0 else cross

    def store_planes(back_y, ids):
        n = len(ids)
        back_x = dot(tix, stack_rows(jnp.concatenate(back_y, axis=1)))
        for k, kz in enumerate(ids):
            part = back_x[:, k * LANES : (k + 1) * LANES]
            corr = part[:BRICK] + sign * pltpu.roll(part[BRICK:], BRICK, 1)
            even, odd_x = corr[: BRICK // 2], corr[BRICK // 2 :]
            qs[pl.ds(kz, BRICK // 2, stride=STEP), :] = jnp.where(
                low_quarter, even, pltpu.roll(odd_x, BRICK, 1)
            )
            if 0 < kz < 32:
                qs[pl.ds(32 + kz, BRICK // 2, stride=STEP), :] = jnp.where(
                    low_quarter, pltpu.roll(even, BRICK, 1), odd_x
                )

    ids = range(BRICK // 2 + 1)
    spec = dot(stack_lanes(jnp.concatenate([load_plane(kz) for kz in ids], axis=0)), ty)
    cross = [cross_of(spec[BRICK * kz : BRICK * (kz + 1)], kz) for kz in ids]
    back_y = dot(jnp.concatenate(split(jnp.concatenate(cross, axis=0)), axis=1), tiy)
    back_y = back_y[:, :LANES] + back_y[:, LANES:]
    back_y = [back_y[BRICK * kz : BRICK * (kz + 1)] for kz in ids]
    for kz in range(0, len(ids), 2):
        store_planes(back_y[kz : kz + 2], ids[kz : kz + 2])

    copies = []
    for x in range(BRICK // 4):
        data = jnp.concatenate(
            [qs[STEP * k : STEP * k + BRICK, :] for k in (2 * x, 2 * x + 1)], axis=1
        )
        result[:, 2 * x * LANES : 2 * (x + 1) * LANES] = dot(tiz, stack_rows(data))
        if x % 4 == 3:
            chunk = pl.ds((x // 4) * 8 * LANES, 8 * LANES)
            copies.append(pltpu.make_async_copy(result.at[:, chunk], out_ref.at[:, chunk], done.at[x // 4]))
            copies[-1].start()
    for copy in copies:
        copy.wait()


def halves(table):
    high = table.astype(ml_dtypes.bfloat16)
    low = (table - high.astype(np.float64)).astype(ml_dtypes.bfloat16)
    return high, low


@functools.cache
def tables():
    wave = np.arange(BRICK)
    angle = 2.0 * np.pi / BRICK * (wave[:, None] * wave[None, :] % BRICK)
    cos, sin = np.cos(angle) / 8.0, np.sin(angle) / 8.0
    high, low = halves(np.concatenate([cos[:33], -sin[1:32]], axis=0))
    fz = np.concatenate([high, high, low], axis=1)
    eye = np.eye(2)
    cos2, sin2 = np.kron(eye, cos), np.kron(eye, sin)
    high, low = halves(np.block([[cos2, -sin2], [sin2, cos2]]))
    ty = np.concatenate([high, high, low], axis=0)
    high, low = halves(np.concatenate([cos, sin], axis=0))
    cs = np.concatenate([high, high, low], axis=1)
    return fz, ty, cs


def per_device(images, offsets, fractions, shifts):
    hbm = pl.BlockSpec(memory_space=pltpu.HBM)
    result = pl.pallas_call(
        exchange_kernel,
        out_shape=jax.ShapeDtypeStruct((BRICK // 2, BRICK * BRICK), F32),
        in_specs=[hbm] * 7,
        out_specs=hbm,
        scratch_shapes=[
            pltpu.SMEM((4, 4), jnp.int32),
            pltpu.SMEM((4, 4), F32),
            pltpu.SMEM((1, 3), jnp.int32),
            pltpu.VMEM((4, 2 * BRICK, LANES), F32),
            pltpu.VMEM((2, MAIN, LANES), F32),
            pltpu.VMEM((2, 2 * BRICK, LANES), F32),
            pltpu.VMEM((MAIN, LANES), F32),
            pltpu.VMEM((2, 2, COLS_R, LANES), F32),
            *[pltpu.VMEM(shape, dtype) for shape, dtype in HANDED + TABLES],
            pltpu.VMEM((BRICK, COLS_V * LANES), F32),
            pltpu.VMEM((8, COLS_U * LANES), F32),
            pltpu.VMEM((16, COLS_U * LANES), BF16),
            pltpu.VMEM((16, COLS_U * LANES), BF16),
            pltpu.VMEM((BRICK * STEP, LANES), F32),
            pltpu.VMEM((BRICK // 2 * STEP, LANES), F32),
            pltpu.VMEM((BRICK // 2, BRICK * BRICK), F32),
            pltpu.SemaphoreType.DMA((4,)),
            pltpu.SemaphoreType.DMA((8,)),
            pltpu.SemaphoreType.DMA((16,)),
            pltpu.SemaphoreType.DMA((16,)),
            pltpu.SemaphoreType.DMA((4,)),
            pltpu.SemaphoreType.DMA((4,)),
        ],
        compiler_params=pltpu.CompilerParams(
            collective_id=0, has_side_effects=True, vmem_limit_bytes=VMEM_LIMIT
        ),
    )(offsets, fractions, shifts, images, *[jnp.asarray(table) for table in tables()])
    return result[None]


def solution(mesh):
    placed = (
        P("exp", None, "tile", None),
        P(None, "depth"),
        P(None, "depth"),
        P(("tile", "depth"), None),
    )
    return jax.shard_map(
        per_device,
        mesh=mesh,
        in_specs=placed,
        out_specs=P(("tile", "depth"), "exp", None),
        check_vma=False,
    )
```

```python
import functools
import math

import jax
import jax.numpy as jnp
import ml_dtypes
import numpy as np
from jax import lax
from jax.experimental import pallas as pl
from jax.experimental.pallas import tpu as pltpu
from jax.sharding import PartitionSpec as P

MESH = pl.DeviceIdType.MESH
BRICK = 64
LANES = 128
EDGE = 24
COLS_R = BRICK + 2 * EDGE
COLS_V = BRICK + 32
COLS_U = BRICK + 16
MAIN = BRICK + EDGE
PEERS = 16
FLOOR = 0.01
STEP = 72
F32 = jnp.float32
BF16 = jnp.bfloat16
VMEM_LIMIT = 60 * 1024 * 1024
HANDED = [
    ((PEERS, 8, LANES), F32),
    ((8 * COLS_R, LANES), F32),
    ((16, COLS_R * LANES), BF16),
    ((16, COLS_R * LANES), BF16),
    ((2 * BRICK, 3 * BRICK), BF16),
    ((4 * BRICK, 2 * LANES), BF16),
    ((BRICK // 2, 3 * BRICK), BF16),
]
TABLES = [((BRICK, 3 * BRICK), BF16), ((12 * BRICK, 4 * BRICK), BF16), ((2 * BRICK, 3 * BRICK), BF16)]


def split(value):
    high = value.astype(BF16)
    low = (value - high.astype(F32)).astype(BF16)
    return high, low


def stack_rows(value):
    high, low = split(value)
    return jnp.concatenate([high, low, high], axis=0)


def stack_lanes(value):
    high, low = split(value)
    return jnp.concatenate([high, low, high], axis=1)


def twice(value):
    high, low = split(value)
    return jnp.concatenate([high, low[:, :BRICK]], axis=1)


def dot(left, right):
    return jnp.dot(left, right, preferred_element_type=F32)


def turn_cos(turns):
    return jnp.cos((turns & (BRICK - 1)).astype(F32) * (2.0 * math.pi / BRICK)) * 0.125


def iota(shape, axis):
    return lax.broadcasted_iota(jnp.int32, shape, axis)


def exchange_kernel(
    off_hbm, frac_hbm, shift_hbm, img_ref, fz_hbm, ty_hbm, cs_hbm, out_ref, off_ref, frac_ref, shift_ref, stage, stage_far, own, far, packed,
    par_ref, r8, rh, rl, tix_ref, tiy_ref, tiz_ref, fz_ref, ty_ref, cs_ref,
    g, a8, uh, ul, zs, qs, result, done, local, p_send, p_recv, i_send, i_recv,
):
    e = lax.axis_index("exp")
    t = lax.axis_index("tile")
    d = lax.axis_index("depth")
    tiles = lax.axis_size("tile")
    other = 1 - e
    yy, zh = d // 4, lax.rem(d, 4)
    half = d // 8
    side = 2 * e - 1

    def depth_of(y, z):
        return lax.rem(y, 4) * 4 + lax.rem(z + 4, 4)

    d_far = depth_of(yy, zh + side)
    t_to = lax.rem(t + 1 - 2 * half + tiles, tiles)
    t_from = lax.rem(t - 1 + 2 * half + tiles, tiles)
    leads = lax.rem(t, 2) == 1
    sibling = t + 1 - 2 * lax.rem(t, 2)
    z_to = [(e, zh), (other, zh + side), (e, zh + side), (other, zh + 2)]
    z_from = [(e, zh), (other, zh + side), (e, zh - side), (other, zh + 2)]
    pairs = sorted([(k, j) for k in range(4) for j in range(4) if k or j], key=lambda p: -p[0] - min(p[1], 4 - p[1]))
    slab_to = [(z_to[k][0], t, depth_of(yy + j, z_to[k][1])) for k, j in pairs]
    slab_from = [(z_from[k][0], t, depth_of(yy + 4 - j, z_from[k][1])) for k, j in pairs]
    images_from = [(other, t, d), (other, t, d_far), (e, t_from, d), (other, t_from, d)]

    small = [
        pltpu.make_async_copy(off_hbm, off_ref, local.at[0]),
        pltpu.make_async_copy(frac_hbm, frac_ref, local.at[1]),
        pltpu.make_async_copy(shift_hbm, shift_ref, local.at[2]),
    ]
    for copy in small:
        copy.start()
    barrier = pltpu.get_barrier_semaphore()

    def greet(devices):
        for device in devices:
            pl.semaphore_signal(barrier, inc=1, device_id=device, device_id_type=MESH)

    @pl.when(leads)
    def _():
        greet(slab_from)

    greet(images_from)

    @pl.when(jnp.logical_not(leads))
    def _():
        greet([(e, sibling, d)])

    def lanes_of(depth):
        return pl.ds(pl.multiple_of(lax.rem(depth, 8) // 2 * LANES, LANES), LANES)

    main_src = pl.ds(pl.multiple_of((BRICK - EDGE) * half, 8), MAIN)
    main_dst = pl.ds(pl.multiple_of(EDGE * (1 - half), 8), MAIN)
    strip_src = pl.ds(pl.multiple_of((2 * BRICK - EDGE) * (1 - half), 8), EDGE)
    strip_dst = pl.ds(pl.multiple_of(MAIN * half, 8), EDGE)

    large = [
        pltpu.make_async_copy(img_ref.at[0, :, :, lanes_of(d)], stage, local.at[3]),
        pltpu.make_async_copy(img_ref.at[0, pl.ds(2, 2), main_src, lanes_of(d_far)], stage_far, local.at[4]),
    ]
    constants = [
        pltpu.make_async_copy(source, target, local.at[5 + k])
        for k, (source, target) in enumerate([(fz_hbm, fz_ref), (ty_hbm, ty_ref), (cs_hbm, cs_ref)])
    ]
    for copy in large + constants:
        copy.start()
    small[0].wait()
    small[1].wait()

    row = iota((8, LANES), 0)
    cam = iota((8, LANES), 1) % 4
    tile = jnp.zeros((8, LANES), F32)
    for c in range(4):
        for z in range(4):
            tile = jnp.where((row == z) & (cam == c), off_ref[c, z].astype(F32), tile)
            tile = jnp.where((row == z + 4) & (cam == c), frac_ref[c, z], tile)
    @pl.when(leads)
    def _():
        par_ref[d] = tile

    def remote(source, target, sends, recvs, index, device):
        return pltpu.make_async_remote_copy(
            src_ref=source,
            dst_ref=target,
            send_sem=sends.at[index],
            recv_sem=recvs.at[index],
            device_id=device,
            device_id_type=MESH,
        )

    slabs = [remote(par_ref.at[d], par_ref.at[d], p_send, p_recv, k, to) for k, to in enumerate(slab_to)]
    handed = remote(par_ref, par_ref, p_send, p_recv, 15, (e, sibling, d))

    pixels = [
        remote(own.at[:, strip_src, :], packed.at[e, :, strip_dst, :], i_send, i_recv, 0, (e, t_to, d)),
        remote(own.at[:, strip_src, :], packed.at[e, :, strip_dst, :], i_send, i_recv, 1, (other, t_to, d)),
        remote(own.at[0, main_src, :], packed.at[e, 0, main_dst, :], i_send, i_recv, 2, (other, t, d)),
        remote(far, packed.at[e, 1, main_dst, :], i_send, i_recv, 3, (other, t, d_far)),
    ]

    @pl.when(leads)
    def _():
        pl.semaphore_wait(barrier, len(slab_to) + 5)
        for copy in slabs:
            copy.start()

    @pl.when(jnp.logical_not(leads))
    def _():
        pl.semaphore_wait(barrier, 4)


    def pack(even, odd, high_half):
        low = iota(even.shape, 1) < BRICK
        kept = jnp.where(high_half, odd, even)
        moved = pltpu.roll(jnp.where(high_half, even, odd), BRICK, 1)
        return jnp.log(jnp.where(low != high_half, kept, moved))

    for copy in large:
        copy.wait()
    for pair in range(2):
        own[pair] = pack(stage[2 * pair], stage[2 * pair + 1], lax.rem(d, 2) == 1)
    far[...] = pack(stage_far[0], stage_far[1], lax.rem(d_far, 2) == 1)
    for copy in pixels:
        copy.start()
    packed[e, :, main_dst, :] = own[:, main_src, :]

    small[2].wait()
    sz, sx, sy = shift_ref[0, 0], shift_ref[0, 1], shift_ref[0, 2]
    r = iota((2 * BRICK, LANES), 0)
    c = iota((2 * BRICK, LANES), 1)
    y_high, y_low = split(turn_cos((r % BRICK) * (c % BRICK + sy) + 16 * (r // BRICK - c // BRICK)))
    zero = jnp.zeros_like(y_low)
    tiy_ref[...] = jnp.concatenate(
        [jnp.concatenate([y_high, y_low], axis=1), jnp.concatenate([y_high, zero], axis=1)], axis=0
    )
    x_of = 2 * (r % (BRICK // 2)) + (r % BRICK) // (BRICK // 2)
    tix_ref[...] = twice(turn_cos((c % BRICK) * (x_of + sx) - 16 * (r // BRICK)))
    r = iota((BRICK // 2, LANES), 0)
    c = iota((BRICK // 2, LANES), 1) % BRICK
    kz = jnp.where(c > 32, c - 32, c)
    weight = jnp.where((kz == 0) | (kz == 32), 1.0, 2.0)
    tiz_ref[...] = twice(weight * turn_cos(kz * (r + 32 * e + sz) + jnp.where(c > 32, 16, 0)))

    for copy in pixels:
        copy.wait_recv()

    low = iota((COLS_R, LANES), 1) < BRICK
    for pair in range(2):
        one, two = packed[0, pair], packed[1, pair]
        both = [
            jnp.where(low, one, pltpu.roll(two, BRICK, 1)),
            jnp.where(low, pltpu.roll(one, BRICK, 1), two),
        ]
        for k in range(2):
            c = 2 * pair + k
            r8[c * COLS_R : (c + 1) * COLS_R, :] = both[k]
            r8[(c + 4) * COLS_R : (c + 5) * COLS_R, :] = pltpu.roll(both[k], COLS_R - 1, 0)
    for x in range(COLS_R - 2):
        col = jnp.concatenate(
            [r8[pl.ds(x, 8, stride=COLS_R), :], r8[pl.ds(x + 2, 8, stride=COLS_R), :]], axis=0
        )
        high, lows = split(col)
        rh[:, x * LANES : (x + 1) * LANES] = high
        rl[:, x * LANES : (x + 1) * LANES] = lows

    @pl.when(leads)
    def _():
        for copy in slabs:
            copy.wait_recv()
        handed.start()

    @pl.when(jnp.logical_not(leads))
    def _():
        handed.wait_recv()

    for copy in constants:
        copy.wait()
    compute_part(
        out_ref, par_ref, r8, rh, rl, tix_ref, tiy_ref, tiz_ref, fz_ref, ty_ref, cs_ref,
        g, a8, uh, ul, zs, qs, result, done,
    )

    @pl.when(leads)
    def _():
        for copy in slabs + [handed]:
            copy.wait_send()

    for copy in pixels:
        copy.wait_send()


def compute_part(
    out_ref, par_ref, r8, rh, rl, tix_ref, tiy_ref, tiz_ref, fz_ref, ty_ref, cs_ref,
    g, a8, uh, ul, zs, qs, result, done,
):
    sub = iota((8, LANES), 0)
    offs, fracs = [], []
    for i in range(PEERS // 2):
        a, b = par_ref[2 * i], par_ref[2 * i + 1]
        offs.append(jnp.where(sub < 4, a, pltpu.roll(b, 4, 0)))
        fracs.append(jnp.where(sub < 4, pltpu.roll(a, 4, 0), b))
    off = jnp.concatenate(offs, axis=0)
    frac = jnp.concatenate(fracs, axis=0)
    s_of = iota((BRICK, LANES), 1) % BRICK // 4 - 7

    def tent(distance):
        return jnp.maximum(0.0, 1.0 - jnp.abs(distance - frac) / 1.5)

    total = tent(-2.0)
    for tap in range(-1, 4):
        total = total + tent(float(tap))
    weights = tent(s_of.astype(F32) - off) / total * 0.25
    back = twice(weights)
    turned = jnp.concatenate([weights, weights], axis=0).T[:BRICK] * 0.0625
    forward = twice(turned)
    ones = jnp.sum(turned[:, :BRICK], axis=1, keepdims=True)
    first = ones[0:8]
    for i in range(1, 8):
        first = first + ones[8 * i : 8 * i + 8]
    first = first + pltpu.roll(jnp.broadcast_to(first, (8, LANES)), 4, 0)
    log_first = jnp.log(first)
    by_lane = jnp.broadcast_to(jnp.sum(weights, axis=0, keepdims=True) * 0.0625, (8, LANES))
    for step in (4, 8, 16, 32):
        by_lane = by_lane + pltpu.roll(by_lane, step, 1)
    lift = jnp.sum(weights * jnp.log(by_lane[0:1]), axis=1, keepdims=True) * 0.5
    lift = jnp.broadcast_to(lift, (BRICK, 2 * LANES))

    def windows(high_ref, low_ref, x):
        def of(ref):
            return [ref[:, (x + 1 + 4 * q) * LANES : (x + 3 + 4 * q) * LANES] for q in range(4)]

        high = of(high_ref)
        return jnp.concatenate(high + of(low_ref) + high, axis=0)

    for x in range(0, COLS_V, 2):
        volume = jnp.exp(dot(back, windows(rh, rl, x)) - lift)
        g[:, x * LANES : (x + 2) * LANES] = dot(forward, stack_rows(volume))

    chunk = 8
    for u in range(0, COLS_U, chunk):
        n = (chunk + 1) * LANES

        def group(row, shift):
            total = None
            for q in range(4):
                start = (u + shift + 12 - 4 * q) * LANES
                part = g[16 * q + row : 16 * q + row + 8, start : start + n]
                total = part if total is None else total + part
            return total

        pairs = group(0, 2) + group(8, 0)
        proj = pairs[:, LANES:] + pltpu.roll(pairs[:, : chunk * LANES], 4, 0)
        log_proj = jnp.log(proj)
        for i in range(chunk):
            ratio = r8[pl.ds(u + i + 16, 8, stride=COLS_R), :]
            a8[:, (u + i) * LANES : (u + i + 1) * LANES] = (
                2.0 * ratio - log_first - log_proj[:, i * LANES : (i + 1) * LANES]
            )

    def column(u):
        return a8[:, u * LANES : (u + 1) * LANES]

    def pair(u):
        return jnp.where(sub < 4, column(u), pltpu.roll(column(u + 1), 4, 0))

    for u in range(COLS_U - 3):
        high, low = split(jnp.concatenate([pair(u), pair(u + 2)], axis=0))
        uh[:, u * LANES : (u + 1) * LANES] = high
        ul[:, u * LANES : (u + 1) * LANES] = low

    fz = fz_ref[...]

    for x in range(0, BRICK, 2):
        volume = jnp.exp(dot(back, windows(uh, ul, x)))
        spec = dot(fz, stack_rows(volume))
        zs[x * STEP : x * STEP + BRICK, :] = spec[:, :LANES]
        zs[(x + 1) * STEP : (x + 1) * STEP + BRICK, :] = spec[:, LANES:]

    ty = ty_ref[...]
    tix, tiy, tiz = tix_ref[...], tiy_ref[...], tiz_ref[...]
    cs = cs_ref[...]
    low_half = iota((BRICK, LANES), 1) < BRICK
    low_quarter = iota((BRICK // 2, LANES), 1) < BRICK
    sign = jnp.where(low_half, -1.0, 1.0)
    row_zero = (iota((BRICK, LANES), 0) == 0) & (iota((BRICK, LANES), 1) % BRICK == 0)

    def load_plane(kz):
        re = zs[pl.ds(kz, BRICK, stride=STEP), :]
        if 0 < kz < 32:
            im = zs[pl.ds(32 + kz, BRICK, stride=STEP), :]
        else:
            im = jnp.zeros_like(re)
        return jnp.concatenate([re, im], axis=1)

    def cross_of(spec, kz):
        spec = dot(cs, stack_rows(spec))
        s_re = spec[:BRICK, :LANES] + spec[BRICK:, LANES:]
        s_im = spec[:BRICK, LANES:] - spec[BRICK:, :LANES]
        m_re = pltpu.roll(s_re, BRICK, 1)
        m_im = pltpu.roll(s_im, BRICK, 1)
        inv = jnp.minimum(
            lax.rsqrt((s_re * s_re + s_im * s_im) * (m_re * m_re + m_im * m_im)), 1.0 / FLOOR
        )
        prod = jnp.where(low_half, s_re * m_re + s_im * m_im, s_im * m_re - s_re * m_im)
        cross = prod * inv
        return jnp.where(row_zero, 0.0, cross) if kz == 0 else cross

    def store_planes(back_y, ids):
        n = len(ids)
        back_x = dot(tix, stack_rows(jnp.concatenate(back_y, axis=1)))
        for k, kz in enumerate(ids):
            part = back_x[:, k * LANES : (k + 1) * LANES]
            corr = part[:BRICK] + sign * pltpu.roll(part[BRICK:], BRICK, 1)
            even, odd_x = corr[: BRICK // 2], corr[BRICK // 2 :]
            qs[pl.ds(kz, BRICK // 2, stride=STEP), :] = jnp.where(
                low_quarter, even, pltpu.roll(odd_x, BRICK, 1)
            )
            if 0 < kz < 32:
                qs[pl.ds(32 + kz, BRICK // 2, stride=STEP), :] = jnp.where(
                    low_quarter, pltpu.roll(even, BRICK, 1), odd_x
                )

    ids = range(BRICK // 2 + 1)
    spec = dot(stack_lanes(jnp.concatenate([load_plane(kz) for kz in ids], axis=0)), ty)
    cross = [cross_of(spec[BRICK * kz : BRICK * (kz + 1)], kz) for kz in ids]
    back_y = dot(jnp.concatenate(split(jnp.concatenate(cross, axis=0)), axis=1), tiy)
    back_y = back_y[:, :LANES] + back_y[:, LANES:]
    back_y = [back_y[BRICK * kz : BRICK * (kz + 1)] for kz in ids]
    for kz in range(0, len(ids), 2):
        store_planes(back_y[kz : kz + 2], ids[kz : kz + 2])

    copies = []
    for x in range(BRICK // 4):
        data = jnp.concatenate(
            [qs[STEP * k : STEP * k + BRICK, :] for k in (2 * x, 2 * x + 1)], axis=1
        )
        result[:, 2 * x * LANES : 2 * (x + 1) * LANES] = dot(tiz, stack_rows(data))
        if x % 4 == 3:
            chunk = pl.ds((x // 4) * 8 * LANES, 8 * LANES)
            copies.append(pltpu.make_async_copy(result.at[:, chunk], out_ref.at[:, chunk], done.at[x // 4]))
            copies[-1].start()
    for copy in copies:
        copy.wait()


def halves(table):
    high = table.astype(ml_dtypes.bfloat16)
    low = (table - high.astype(np.float64)).astype(ml_dtypes.bfloat16)
    return high, low


@functools.cache
def tables():
    wave = np.arange(BRICK)
    angle = 2.0 * np.pi / BRICK * (wave[:, None] * wave[None, :] % BRICK)
    cos, sin = np.cos(angle) / 8.0, np.sin(angle) / 8.0
    high, low = halves(np.concatenate([cos[:33], -sin[1:32]], axis=0))
    fz = np.concatenate([high, high, low], axis=1)
    eye = np.eye(2)
    cos2, sin2 = np.kron(eye, cos), np.kron(eye, sin)
    high, low = halves(np.block([[cos2, -sin2], [sin2, cos2]]))
    ty = np.concatenate([high, high, low], axis=0)
    high, low = halves(np.concatenate([cos, sin], axis=0))
    cs = np.concatenate([high, high, low], axis=1)
    return fz, ty, cs


def per_device(images, offsets, fractions, shifts):
    hbm = pl.BlockSpec(memory_space=pltpu.HBM)
    result = pl.pallas_call(
        exchange_kernel,
        out_shape=jax.ShapeDtypeStruct((BRICK // 2, BRICK * BRICK), F32),
        in_specs=[hbm] * 7,
        out_specs=hbm,
        scratch_shapes=[
            pltpu.SMEM((4, 4), jnp.int32),
            pltpu.SMEM((4, 4), F32),
            pltpu.SMEM((1, 3), jnp.int32),
            pltpu.VMEM((4, 2 * BRICK, LANES), F32),
            pltpu.VMEM((2, MAIN, LANES), F32),
            pltpu.VMEM((2, 2 * BRICK, LANES), F32),
            pltpu.VMEM((MAIN, LANES), F32),
            pltpu.VMEM((2, 2, COLS_R, LANES), F32),
            *[pltpu.VMEM(shape, dtype) for shape, dtype in HANDED + TABLES],
            pltpu.VMEM((BRICK, COLS_V * LANES), F32),
            pltpu.VMEM((8, COLS_U * LANES), F32),
            pltpu.VMEM((16, COLS_U * LANES), BF16),
            pltpu.VMEM((16, COLS_U * LANES), BF16),
            pltpu.VMEM((BRICK * STEP, LANES), F32),
            pltpu.VMEM((BRICK // 2 * STEP, LANES), F32),
            pltpu.VMEM((BRICK // 2, BRICK * BRICK), F32),
            pltpu.SemaphoreType.DMA((4,)),
            pltpu.SemaphoreType.DMA((8,)),
            pltpu.SemaphoreType.DMA((16,)),
            pltpu.SemaphoreType.DMA((16,)),
            pltpu.SemaphoreType.DMA((4,)),
            pltpu.SemaphoreType.DMA((4,)),
        ],
        compiler_params=pltpu.CompilerParams(
            collective_id=0, has_side_effects=True, vmem_limit_bytes=VMEM_LIMIT
        ),
    )(offsets, fractions, shifts, images, *[jnp.asarray(table) for table in tables()])
    return result[None]


def solution(mesh):
    placed = (
        P("exp", None, "tile", None),
        P(None, "depth"),
        P(None, "depth"),
        P(("tile", "depth"), None),
    )
    return jax.shard_map(
        per_device,
        mesh=mesh,
        in_specs=placed,
        out_specs=P(("tile", "depth"), "exp", None),
        check_vma=False,
    )
```
